512 devices in a mesh: seq: 128 (over z_hi, x, y, core), head: 4 (over z_lo).
Axes of the slice: x: 4, y: 4, z: 16 (z_hi: 4, z_lo: 4; z = z_hi * 4 + z_lo), core: 2. Of those that a mesh axis runs over, the one named last changes fastest.
Arguments:
- tokens: bfloat16 [49152, 768], P(('seq', 'head')), may hold values from -6 to 6
- norm_gain: float32 [768], replicated, may hold values from 0.5 to 1.5
- qkv_weight: bfloat16 [3, 12, 64, 768], P(None, 'head'), may hold values from -1 to 1
- out_weight: bfloat16 [768, 768], replicated, may hold values from -0.21875 to 0.21875
- dec_weight: bfloat16 [256, 3, 3, 768], P('head'), may hold values from -0.078125 to 0.078125
- offsets: int32 [3, 12], replicated, may hold values from 0 to 127, as said below
Outputs:
- layer: bfloat16 [49152, 768], P(('seq', 'head'))
- decoded: bfloat16 [256, 128, 384], P('head', 'seq')
The draws below stay inside these ranges and needn't reach their ends.
Inputs may be any that keep to these rules, and one draw needn't show every extreme that they name: offsets[0, h], offsets[1, h] and offsets[2, h] lie below 4, 8 and 128 respectively; in each of the three rows some head takes that row's largest offset and some other head takes 0.
All inputs are finite; a program needn't handle non-finite values.
Results may differ from the reference program's by a relative error of at most 0.012.
Values may be sent and summed in bfloat16 or wider, within the bound.
A program may use at most 64 MiB of HBM per device.

```python
import math
import jax
import jax.numpy as jnp
from jax import lax

D = 768
HEADS = 12
HEAD_DIM = 64
C_DEC = 256
GRID_W = 384
GROUP2 = 4
GROUP3 = 8
TOK_DEV = 384
TOKENS = 49152
GRID_H = 128
GROUP4 = 128


def draw_qkv_weight(key, part):
    key = jax.random.fold_in(key, 7)
    key_base = jax.random.fold_in(key, 0)
    spread = 2.0 / math.sqrt(D)
    base = jax.random.normal(key_base, (3, HEADS, HEAD_DIM, D), jnp.float32) * spread
    return jnp.clip(base, -1.0, 1.0).astype(jnp.bfloat16)


def draw_offsets(key, part):
    key = jax.random.fold_in(key, 5)
    key_values, key_top, key_low = jax.random.split(key, 3)
    raw_values = jax.random.randint(key_values, (3, HEADS), 0, 1048576, jnp.int32)
    spans = jnp.array([GROUP2, GROUP3, GROUP4], jnp.int32)
    values = raw_values % spans[:, None]
    top_pick = jax.random.randint(key_top, (3,), 0, HEADS, jnp.int32)
    low_step = jax.random.randint(key_low, (3,), 1, HEADS, jnp.int32)
    low_pick = (top_pick + low_step) % HEADS
    head_ids = jnp.arange(HEADS, dtype=jnp.int32)
    values = jnp.where(head_ids[None, :] == top_pick[:, None], spans[:, None] - 1, values)
    values = jnp.where(head_ids[None, :] == low_pick[:, None], 0, values)
    return values.astype(jnp.int32)


def level_of(key, extent, shards, smallest, top_value):
    loudness, own = 1.0, jax.random.fold_in(key, 6)
    for position, blocks in shards:
        draws = jnp.exp(jax.random.uniform(jax.random.fold_in(own, position), (blocks,), jnp.float32, smallest / len(shards), top_value / len(shards)))
        loudness = loudness * jnp.repeat(draws, extent[position] // blocks).reshape([-1 if axis == position else 1 for axis in range(len(extent))])
    return loudness


def bell_draw(stream_key, extent, width, bound, shards=(), held_as=jnp.bfloat16):
    drawn = jax.random.normal(stream_key, extent, jnp.float32) * width
    if len(shards) > 0:
        drawn = level_of(stream_key, extent, shards, -0.22, 0.18) * drawn
    return jnp.clip(drawn, min=-bound, max=bound).astype(held_as)


def setup_inputs(seed: int = 0) -> dict:
    splits = jax.random.split(jax.random.key(seed), 7)
    return {
        "tokens": bell_draw(splits[0], (TOKENS, D), 1.0, 6.0, ((0, 512),)),
        "norm_gain": jnp.clip(1.0 + 0.1 * jax.random.normal(splits[1], (D,), jnp.float32), 0.5, 1.5),
        "qkv_weight": draw_qkv_weight(jax.random.fold_in(splits[6], 71), 0),
        "out_weight": bell_draw(splits[3], (D, D), D ** -0.5, 0.21875),
        "dec_weight": bell_draw(splits[4], (C_DEC, 3, 3, D), (9 * D) ** -0.5, 0.078125, ((0, 4),)),
        "offsets": draw_offsets(jax.random.fold_in(splits[6], 71), 0),
    }


def layer_norm(token_rows, norm_scale):
    values = token_rows.astype(jnp.float32)
    centred = values - lax.optimization_barrier(jnp.mean(values, -1, keepdims=True))
    spread = lax.optimization_barrier(jnp.mean(centred * centred, -1, keepdims=True))
    return (centred * lax.rsqrt(spread + 1e-06) * norm_scale).astype(jnp.bfloat16)

def attend(queries, key_rows, value_rows):
    scores = jnp.einsum('hqd,hkd->hqk', queries.astype(jnp.float32), key_rows.astype(jnp.float32)) * HEAD_DIM ** (-0.5)
    row_peak = lax.optimization_barrier(jnp.max(scores, -1, keepdims=True))
    exp_terms = jnp.exp(scores - row_peak)
    totals = lax.optimization_barrier(jnp.sum(exp_terms, -1))
    prob_weights = lax.optimization_barrier(exp_terms.astype(jnp.bfloat16)).astype(jnp.float32)
    summed = jnp.einsum('hqk,hkd->hqd', prob_weights, value_rows.astype(jnp.float32))
    return (summed / totals[..., None], row_peak[..., 0] + jnp.log(totals))

def branch(qkv_head, group, offset):
    set_count = TOKENS // (group * TOK_DEV)
    shaped = qkv_head.reshape(set_count, TOK_DEV, group, 3, HEAD_DIM)
    chosen = lax.dynamic_index_in_dim(shaped, offset, 2, keepdims=False)

    def per_set(member):
        return attend(member[None, :, 0], member[None, :, 1], member[None, :, 2])
    outputs, lse_sets = lax.map(per_set, chosen)
    outputs = outputs[:, 0]
    lse_sets = lse_sets[:, 0]
    hit_marks = jnp.arange(group, dtype=jnp.int32) == offset
    full_out = (outputs[:, :, None, :] * hit_marks.astype(jnp.float32)[None, None, :, None]).reshape(TOKENS, HEAD_DIM)
    cover = jnp.broadcast_to(hit_marks[None, None, :], (set_count, TOK_DEV, group)).reshape(TOKENS)
    lse_full = jnp.broadcast_to(lse_sets[:, :, None], (set_count, TOK_DEV, group)).reshape(TOKENS)
    return (full_out, lse_full, cover)

def reference(tokens, norm_gain, qkv_weight, out_weight, dec_weight, offsets):
    normed = layer_norm(tokens, norm_gain)
    head_ids = jnp.arange(HEADS, dtype=jnp.int32)

    def one_head(head_idx):
        rows_of_head = lax.dynamic_index_in_dim(qkv_weight, head_idx, 1, keepdims=False)
        qkv_head = jnp.dot(normed, jnp.transpose(rows_of_head.reshape(3 * HEAD_DIM, D)), preferred_element_type=jnp.float32)
        qkv_head = lax.optimization_barrier(qkv_head.astype(jnp.bfloat16)).reshape(TOKENS, 3, HEAD_DIM)
        head_offsets = lax.dynamic_index_in_dim(offsets, head_idx, 1, keepdims=False)
        out_one, lse_one, cover_one = branch(qkv_head, 1, jnp.zeros((), jnp.int32))
        others = [branch(qkv_head, GROUP2, head_offsets[0]), branch(qkv_head, GROUP3, head_offsets[1]), branch(qkv_head, GROUP4, head_offsets[2])]
        peak_lse = lse_one
        for full_out, lse_full, cover in others:
            peak_lse = jnp.where(cover, jnp.maximum(peak_lse, lse_full), peak_lse)
        weight_one = jnp.exp(lse_one - peak_lse)
        numerator = weight_one[:, None] * out_one
        denominator = weight_one
        for full_out, lse_full, cover in others:
            weight_branch = jnp.where(cover, jnp.exp(jnp.where(cover, lse_full, peak_lse) - peak_lse), 0.0)
            numerator = numerator + weight_branch[:, None] * full_out
            denominator = denominator + weight_branch
        return (numerator / denominator[:, None]).astype(jnp.bfloat16)
    per_head = lax.map(one_head, head_ids)
    attended = jnp.transpose(per_head, (1, 0, 2)).reshape(TOKENS, D)
    layer = (tokens.astype(jnp.float32) + jnp.dot(attended, out_weight, preferred_element_type=jnp.float32)).astype(jnp.bfloat16)
    grid = layer.reshape(GRID_H, GRID_W, D)
    padded = jnp.pad(grid, ((1, 1), (1, 1), (0, 0)))
    conv = jnp.zeros((GRID_H * GRID_W, C_DEC), jnp.float32)
    for row_tap in range(3):
        for col_tap in range(3):
            window = padded[row_tap:row_tap + GRID_H, col_tap:col_tap + GRID_W, :].reshape(GRID_H * GRID_W, D)
            conv = conv + jnp.dot(window, jnp.transpose(dec_weight[:, row_tap, col_tap, :]), preferred_element_type=jnp.float32)
    decoded = jax.nn.gelu(conv, approximate=False).astype(jnp.bfloat16)
    decoded = jnp.transpose(decoded, (1, 0)).reshape(C_DEC, GRID_H, GRID_W)
    return (layer, decoded)
```

```python
import functools

import jax
import jax.numpy as jnp
from jax import lax
from jax.experimental import pallas as pl
from jax.experimental.pallas import tpu as pltpu
from jax.sharding import PartitionSpec as P

MESH = pl.DeviceIdType.MESH
LOG2E = 1.4426950408889634
SCALE = 0.125 * LOG2E
F32 = jnp.float32
BF16 = jnp.bfloat16


def nt_dot(a, b):
    return lax.dot_general(a, b, (((1,), (1,)), ((), ())), preferred_element_type=F32)


def seq_of(zh, x, y, c):
    return ((zh * 4 + x) * 4 + y) * 2 + c


def layer_norm(rows, gain):
    values = rows.astype(F32)
    centred = values - jnp.mean(values, -1, keepdims=True)
    spread = jnp.mean(centred * centred, -1, keepdims=True)
    return (centred * lax.rsqrt(spread + 1e-06) * gain).astype(BF16)


def attend(q, kv, out_lanes, keep=None):
    scores = nt_dot(q, kv) * SCALE
    if keep is not None:
        scores = jnp.where(keep, scores, -1e30)
    top = jnp.max(scores, -1, keepdims=True)
    terms = jnp.exp2(scores - top)
    total = jnp.sum(terms, -1, keepdims=True)
    out = jnp.dot(terms.astype(BF16), kv, preferred_element_type=F32)
    lse = top + jnp.log(total) * LOG2E
    return jnp.where(out_lanes, out / total, lse)


def body(
    tok, gain, wqkv, wout, wdec, off,
    layer_out, dec_out,
    X, gain_v, WQ, W01, W2, WD, QB, QF,
    S2, B2, S3, B3, S4F, Q4F, G1, G2,
    T1, E2, E3, MR, A01, A2, PF, PT, L, HS, HR, DO,
    in_sem, tok_s, tok_r, b2_s, b2_r, b3_s, b3_r, g1_s, g1_r, g2_s, g2_r,
    a01_s, a01_r, a2_s, a2_r, pt_s, pt_r, h_s, h_r, out_sem,
):
    s = lax.axis_index("seq")
    z = lax.axis_index("head")
    core = lax.rem(s, 2)
    y = lax.rem(lax.div(s, 2), 4)
    x = lax.rem(lax.div(s, 8), 4)
    zh = lax.div(s, 32)
    yc = lax.rem(s, 8)
    zx = lax.div(s, 8)
    quad = lax.rem(s, 4)

    def head_peer(d):
        return (s, lax.rem(z + d, 4))

    def quad_peer(d):
        return (s - quad + lax.rem(quad + d, 4), z)

    def yc_peer(d):
        return (s - yc + lax.rem(yc + d, 8), z)

    def zx_peer(d):
        return (lax.rem(zx + d, 16) * 8 + yc, z)

    up = (lax.rem(s + 1, 128), z)
    down = (lax.rem(s + 127, 128), z)

    barrier = pltpu.get_barrier_semaphore()
    peers = [head_peer(d) for d in range(1, 4)]
    peers += [yc_peer(d) for d in range(1, 8)]
    peers += [zx_peer(d) for d in range(1, 16)]
    peers += [up, down]
    for peer in peers:
        pl.semaphore_signal(barrier, inc=1, device_id=peer, device_id_type=MESH)

    loads = []

    def load(src, dst):
        copy = pltpu.make_async_copy(src, dst, in_sem.at[len(loads)])
        copy.start()
        loads.append(copy)
        return copy

    c_tok = load(tok, X.at[z])
    c_gain = load(gain, gain_v)
    c_qkv = []
    for h in range(3):
        q_at, k_at, v_at = (64, 64, 0) if h == 0 else (0, 0, 64)
        c_qkv.append(load(wqkv.at[pl.ds(64 * h, 64)], WQ.at[pl.ds(128 * h + q_at, 64)]))
        c_qkv.append(load(wqkv.at[pl.ds(192 + 64 * h, 64)], WQ.at[pl.ds(384 + 128 * h + k_at, 64)]))
        c_qkv.append(load(wqkv.at[pl.ds(384 + 64 * h, 64)], WQ.at[pl.ds(384 + 128 * h + v_at, 64)]))
    c_late = [load(wdec, WD)]
    for g in range(4):
        c_late.append(load(wout.at[pl.ds(192 * g, 128)], W01.at[pl.ds(128 * g, 128)]))
        c_late.append(load(wout.at[pl.ds(192 * g + 128, 64)], W2.at[0, pl.ds(128 * g, 64)]))
        c_late.append(load(wout.at[pl.ds(192 * g + 128, 64)], W2.at[1, pl.ds(128 * g + 64, 64)]))
    zero64 = jnp.zeros((64, 768), BF16)
    for h in range(3):
        WQ[pl.ds(128 * h + (0 if h == 0 else 64), 64), :] = zero64
    for g in range(4):
        W2[0, pl.ds(128 * g + 64, 64), :] = zero64
        W2[1, pl.ds(128 * g, 64), :] = zero64
    S4F[...] = jnp.zeros_like(S4F)
    Q4F[...] = jnp.zeros_like(Q4F)

    c_tok.wait()
    pl.semaphore_wait(barrier, len(peers))

    def remote(src, dst, ssem, rsem, peer):
        return pltpu.make_async_remote_copy(
            src_ref=src, dst_ref=dst, send_sem=ssem, recv_sem=rsem,
            device_id=peer, device_id_type=MESH,
        )

    sent = []

    tok_copies = [
        remote(X.at[z], X.at[z], tok_s.at[d], tok_r.at[d], head_peer(d)) for d in range(1, 4)
    ]
    for copy in tok_copies:
        copy.start()
    sent += tok_copies

    c_gain.wait()
    for copy in c_qkv:
        copy.wait()
    gain_row = gain_v[...]

    for d in range(4):
        src = lax.rem(z - d + 4, 4)
        if d:
            remote(X.at[src], X.at[src], tok_s.at[d], tok_r.at[d], head_peer(d)).wait_recv()
        normed = layer_norm(X[src], gain_row)
        rows = pl.ds(pl.multiple_of(src * 96, 96), 96)
        for t in range(6):
            part = nt_dot(normed, WQ[pl.ds(128 * t, 128), :]).astype(BF16)
            QB[t, rows, :] = part
            QF[t, rows, :] = part.astype(F32)

    lane = lax.broadcasted_iota(jnp.int32, (1, 128), 1)
    left = lane < 64
    right = lane >= 64
    out_lanes = (left, right, right)
    o2 = [off[0, 3 * z + h] for h in range(3)]
    o3 = [off[1, 3 * z + h] for h in range(3)]
    o4 = [off[2, 3 * z + h] for h in range(3)]

    for h in range(3):
        for j in range(3):
            S4F[3 * h + j : 3 * h + j + 1, :] = QF[3 + h, pl.ds(o4[h] + 128 * j, 1), :]
            Q4F[3 * h + j : 3 * h + j + 1, :] = QF[h, pl.ds(o4[h] + 128 * j, 1), :]
    G1[zx] = S4F[...].astype(BF16)
    g1_copies = [
        remote(G1.at[zx], G1.at[zx], g1_s.at[d], g1_r.at[d], zx_peer(d)) for d in range(1, 16)
    ]
    for copy in g1_copies:
        copy.start()
    for h in range(3):
        B2[quad, h] = QF[3 + h, pl.ds(o2[h], 96, stride=4), :].astype(BF16)
        B3[yc, h] = QF[3 + h, pl.ds(o3[h], 48, stride=8), :].astype(BF16)
    b2_copies = [
        remote(B2.at[quad], B2.at[quad], b2_s.at[d], b2_r.at[d], quad_peer(d)) for d in range(1, 4)
    ]
    b3_copies = [
        remote(B3.at[yc], B3.at[yc], b3_s.at[d], b3_r.at[d], yc_peer(d)) for d in range(1, 8)
    ]
    for copy in b2_copies + b3_copies:
        copy.start()
    sent += g1_copies + b2_copies + b3_copies

    def branch_one(h):
        kv = QB[3 + h]
        for i in range(3):
            rows = pl.ds(128 * i, 128)
            T1[h, rows, :] = attend(QB[h, rows, :], kv, out_lanes[h])

    branch_one(0)
    branch_one(1)

    for d in range(1, 16):
        src = lax.rem(zx - d + 16, 16)
        remote(G1.at[src], G1.at[src], g1_s.at[d], g1_r.at[d], zx_peer(d)).wait_recv()
    G2[yc] = G1[...]
    g2_copies = [
        remote(G2.at[yc], G2.at[yc], g2_s.at[d], g2_r.at[d], yc_peer(d)) for d in range(1, 8)
    ]
    for copy in g2_copies:
        copy.start()
    sent += g2_copies

    branch_one(2)

    for d in range(1, 4):
        src = lax.rem(quad - d + 4, 4)
        remote(B2.at[src], B2.at[src], b2_s.at[d], b2_r.at[d], quad_peer(d)).wait_recv()

    for h in range(3):
        kv = jnp.concatenate([B2[m, h] for m in range(4)], axis=0)
        q = QF[h, pl.ds(o2[h], 96, stride=4), :].astype(BF16)
        tile = attend(q, kv, out_lanes[h])
        for p in range(4):
            E2[h, pl.ds(p, 96, stride=4), :] = tile

    for d in range(1, 8):
        src = lax.rem(yc - d + 8, 8)
        remote(B3.at[src], B3.at[src], b3_s.at[d], b3_r.at[d], yc_peer(d)).wait_recv()

    def branch_three(h):
        kv = jnp.concatenate([B3[m, h] for m in range(8)], axis=0)
        q = QF[h, pl.ds(o3[h], 48, stride=8), :].astype(BF16)
        tile = attend(q, kv, out_lanes[h])
        for p in range(8):
            E3[h, pl.ds(p, 48, stride=8), :] = tile

    token = lax.broadcasted_iota(jnp.int32, (384, 128), 0)

    def merge(h):
        t1, t2, t3 = T1[h], E2[h], E3[h]
        l1, l2, l3 = (pltpu.roll(t, 64, 1) for t in (t1, t2, t3))
        c2 = (token & 3) == o2[h]
        c3 = (token & 7) == o3[h]
        peak = jnp.where(c2, jnp.maximum(l1, l2), l1)
        peak = jnp.where(c3, jnp.maximum(peak, l3), peak)
        w1 = jnp.exp2(l1 - peak)
        w2 = jnp.where(c2, jnp.exp2(l2 - peak), 0.0)
        w3 = jnp.where(c3, jnp.exp2(l3 - peak), 0.0)
        den = w1 + w2 + w3
        out = (w1 * t1 + w2 * t2 + w3 * t3) / den
        lse = peak + jnp.log(den) * LOG2E
        MR[h] = jnp.where(out_lanes[h], out, pltpu.roll(lse, 64, 1))
        return out

    branch_three(0)
    branch_three(1)
    A01[z] = jnp.where(left, merge(0), merge(1)).astype(BF16)
    a01_copies = [
        remote(A01.at[z], A01.at[z], a01_s.at[d], a01_r.at[d], head_peer(d)) for d in range(1, 4)
    ]
    for copy in a01_copies:
        copy.start()
    branch_three(2)
    m2 = merge(2)
    A2[z] = jnp.where(left, pltpu.roll(m2[:192], 64, 1), m2[192:]).astype(BF16)
    a2_copies = [
        remote(A2.at[z], A2.at[z], a2_s.at[d], a2_r.at[d], head_peer(d)) for d in range(1, 4)
    ]
    for copy in a2_copies:
        copy.start()
    sent += a01_copies + a2_copies

    for d in range(1, 8):
        src = lax.rem(yc - d + 8, 8)
        remote(G2.at[src], G2.at[src], g2_s.at[d], g2_r.at[d], yc_peer(d)).wait_recv()
    kv4 = G2[...].reshape(2048, 128)
    key_row = lax.broadcasted_iota(jnp.int32, (16, 2048), 1) & 15
    query_row = lax.broadcasted_iota(jnp.int32, (16, 2048), 0)

    def head_row(r):
        return jnp.where(r < 3, 0, jnp.where(r < 6, 1, jnp.where(r < 9, 2, 3)))

    keep = head_row(key_row) == head_row(query_row)
    row16 = lax.broadcasted_iota(jnp.int32, (16, 128), 0)
    lane16 = lax.broadcasted_iota(jnp.int32, (16, 128), 1)
    out16 = (row16 < 3) == (lane16 < 64)
    tile4 = attend(Q4F[...].astype(BF16), kv4, out16, keep)
    for h in range(3):
        for j in range(3):
            S4F[3 * h + j : 3 * h + j + 1, :] = MR[h, pl.ds(o4[h] + 128 * j, 1), :]
    tile1 = S4F[...]
    l1 = pltpu.roll(tile1, 64, 1)
    l4 = pltpu.roll(tile4, 64, 1)
    peak = jnp.maximum(l1, l4)
    w1 = jnp.exp2(l1 - peak)
    w4 = jnp.exp2(l4 - peak)
    both = (w1 * tile1 + w4 * tile4) / (w1 + w4)
    turned = pltpu.roll(both, 64, 1)
    PF[...] = jnp.zeros_like(PF)
    PF[0:3, :] = jnp.where(left, both[0:3], both[3:6])
    PF[3:6, :] = jnp.where(left, turned[6:9], both[6:9])
    PT[z] = PF[...].astype(BF16)
    pt_copies = [
        remote(PT.at[z], PT.at[z], pt_s.at[d], pt_r.at[d], head_peer(d)) for d in range(1, 4)
    ]
    for copy in pt_copies:
        copy.start()
    sent += pt_copies

    for copy in c_late:
        copy.wait()

    for d in range(1, 4):
        src = lax.rem(z - d + 4, 4)
        remote(A01.at[src], A01.at[src], a01_s.at[d], a01_r.at[d], head_peer(d)).wait_recv()
        remote(A2.at[src], A2.at[src], a2_s.at[d], a2_r.at[d], head_peer(d)).wait_recv()
        remote(PT.at[src], PT.at[src], pt_s.at[d], pt_r.at[d], head_peer(d)).wait_recv()
    row128 = lax.broadcasted_iota(jnp.int32, (128, 128), 0)
    tok2 = lax.broadcasted_iota(jnp.int32, (192, 128), 0) + jnp.where(left, 0, 192)
    p01, p2 = [], []
    for g in range(4):
        patch = PT[g].astype(F32)
        o_lane = jnp.where(left, off[2, 3 * g], off[2, 3 * g + 1])
        hit = row128 == o_lane
        whole = A01[g].astype(F32)
        p01.append(
            jnp.concatenate(
                [
                    jnp.where(hit, patch[j : j + 1], whole[128 * j : 128 * j + 128])
                    for j in range(3)
                ],
                axis=0,
            ).astype(BF16)
        )
        packed = A2[g].astype(F32)
        for j in range(3):
            packed = jnp.where(tok2 == off[2, 3 * g + 2] + 128 * j, patch[3 + j : 4 + j], packed)
        p2.append(packed.astype(BF16))
    for half in range(2):
        first = jnp.concatenate([p[192 * half : 192 * half + 192] for p in p01], axis=1)
        second = jnp.concatenate(p2, axis=1)
        acc = jnp.dot(first, W01[...], preferred_element_type=F32)
        acc = acc + jnp.dot(second, W2[half], preferred_element_type=F32)
        own = X[2 * half : 2 * half + 2].reshape(192, 768).astype(F32)
        L[192 * half : 192 * half + 192, :] = (own + acc).astype(BF16)
    c_layer = pltpu.make_async_copy(
        L.at[pl.ds(pl.multiple_of(z * 96, 96), 96)], layer_out, out_sem.at[0]
    )
    c_layer.start()

    col = lax.broadcasted_iota(jnp.int32, (64, 384), 1)

    def part(dy):
        p = nt_dot(WD[192 * dy : 192 * dy + 192, :], L[...])
        before = jnp.where(col == 0, 0.0, pltpu.roll(p[0:64], 1, 1))
        after = jnp.where(col == 383, 0.0, pltpu.roll(p[128:192], 383, 1))
        return before + p[64:128] + after

    HS[0] = part(0).astype(BF16)
    h_up = remote(HS.at[0], HR.at[0], h_s.at[0], h_r.at[0], up)
    h_up.start()
    HS[1] = part(2).astype(BF16)
    h_down = remote(HS.at[1], HR.at[1], h_s.at[1], h_r.at[1], down)
    h_down.start()
    middle = part(1)
    h_up.wait_recv()
    h_down.wait_recv()
    conv = middle + jnp.where(s > 0, HR[0].astype(F32), 0.0)
    conv = conv + jnp.where(s < 127, HR[1].astype(F32), 0.0)
    DO[...] = (0.5 * conv * (1.0 + lax.erf(conv * 0.7071067811865476))).astype(BF16)
    c_dec = pltpu.make_async_copy(DO, dec_out, out_sem.at[1])
    c_dec.start()

    for copy in sent + [h_up, h_down]:
        copy.wait_send()
    c_layer.wait()
    c_dec.wait()


def shards(tokens, norm_gain, qkv_weight, out_weight, dec_weight, offsets):
    wqkv = qkv_weight.reshape(576, 768)
    wdec = jnp.transpose(dec_weight, (1, 2, 0, 3)).reshape(576, 768)
    gain = norm_gain.reshape(1, 768)
    vm = pltpu.VMEM
    dma = pltpu.SemaphoreType.DMA
    layer, decoded = pl.pallas_call(
        body,
        out_shape=(
            jax.ShapeDtypeStruct((96, 768), BF16),
            jax.ShapeDtypeStruct((64, 384), BF16),
        ),
        in_specs=[pl.BlockSpec(memory_space=pl.ANY)] * 5
        + [pl.BlockSpec(memory_space=pltpu.SMEM)],
        out_specs=(pl.BlockSpec(memory_space=pl.ANY),) * 2,
        scratch_shapes=[
            vm((4, 96, 768), BF16),
            vm((1, 768), F32),
            vm((768, 768), BF16),
            vm((512, 768), BF16),
            vm((2, 512, 768), BF16),
            vm((576, 768), BF16),
            vm((6, 384, 128), BF16),
            vm((6, 384, 128), F32),
            vm((16, 128), BF16),
            vm((4, 3, 96, 128), BF16),
            vm((16, 128), BF16),
            vm((8, 3, 48, 128), BF16),
            vm((16, 128), F32),
            vm((16, 128), F32),
            vm((16, 16, 128), BF16),
            vm((8, 16, 16, 128), BF16),
            vm((3, 384, 128), F32),
            vm((3, 384, 128), F32),
            vm((3, 384, 128), F32),
            vm((3, 384, 128), F32),
            vm((4, 384, 128), BF16),
            vm((4, 192, 128), BF16),
            vm((16, 128), F32),
            vm((4, 16, 128), BF16),
            vm((384, 768), BF16),
            vm((2, 64, 384), BF16),
            vm((2, 64, 384), BF16),
            vm((64, 384), BF16),
            dma((24,)),
            dma((4,)), dma((4,)),
            dma((4,)), dma((4,)),
            dma((8,)), dma((8,)),
            dma((16,)), dma((16,)),
            dma((8,)), dma((8,)),
            dma((4,)), dma((4,)),
            dma((4,)), dma((4,)),
            dma((4,)), dma((4,)),
            dma((2,)), dma((2,)),
            dma((2,)),
        ],
        compiler_params=pltpu.CompilerParams(
            collective_id=0, has_side_effects=True, vmem_limit_bytes=48 * 1024 * 1024
        ),
        cost_estimate=pl.CostEstimate(
            flops=1500000000, bytes_accessed=4000000, transcendentals=700000
        ),
        name="dilated_layer",
    )(tokens, gain, wqkv, out_weight, wdec, offsets)
    return layer, decoded.reshape(64, 1, 384)


def solution(mesh):
    placed = (
        P(("seq", "head"), None),
        P(),
        P(None, "head", None, None),
        P(),
        P("head", None, None, None),
        P(),
    )
    return jax.shard_map(
        shards,
        mesh=mesh,
        in_specs=placed,
        out_specs=(P(("seq", "head"), None), P("head", "seq", None)),
        check_vma=False,
    )
```

```python
import functools

import jax
import jax.numpy as jnp
from jax import lax
from jax.experimental import pallas as pl
from jax.experimental.pallas import tpu as pltpu
from jax.sharding import PartitionSpec as P

MESH = pl.DeviceIdType.MESH
LOG2E = 1.4426950408889634
SCALE = 0.125 * LOG2E
F32 = jnp.float32
BF16 = jnp.bfloat16


def nt_dot(a, b):
    return lax.dot_general(a, b, (((1,), (1,)), ((), ())), preferred_element_type=F32)


def seq_of(zh, x, y, c):
    return ((zh * 4 + x) * 4 + y) * 2 + c


def layer_norm(rows, gain):
    values = rows.astype(F32)
    centred = values - jnp.mean(values, -1, keepdims=True)
    spread = jnp.mean(centred * centred, -1, keepdims=True)
    return (centred * lax.rsqrt(spread + 1e-06) * gain).astype(BF16)


def attend(q, kv, out_lanes, keep=None):
    scores = nt_dot(q, kv) * SCALE
    if keep is not None:
        scores = jnp.where(keep, scores, -1e30)
    top = jnp.max(scores, -1, keepdims=True)
    terms = jnp.exp2(scores - top)
    total = jnp.sum(terms, -1, keepdims=True)
    out = jnp.dot(terms.astype(BF16), kv, preferred_element_type=F32)
    lse = top + jnp.log(total) * LOG2E
    return jnp.where(out_lanes, out / total, lse)


def body(
    tok, gain, wqkv, wout, wdec, off,
    layer_out, dec_out,
    X, gain_v, WQ, W01, W2, WD, QB, QF,
    BX, S4F, Q4F, G1, G2,
    T1, E2, E3, MR, AA, PF, PT, L, HS, HR, DO,
    in_sem, tok_s, tok_f, tok_r, bx_s, bx_r, g1_s, g1_r, g2_s, g2_r,
    aa_s, aa_f, aa_r, pt_s, pt_r, h_s, h_r, out_sem, lead_sem, go_sem,
):
    s = lax.axis_index("seq")
    z = lax.axis_index("head")
    yc = lax.rem(s, 8)
    zx = lax.div(s, 8)
    quad = lax.rem(s, 4)
    quad_base = yc - quad
    far_base = lax.rem(quad_base + 4, 8)
    s_base = s - yc
    side = lax.div(z, 2)
    u = z + side * (3 - 2 * z)
    inner = (s, z + 1 - 2 * side)
    outer = (s, z - 1 + 2 * side)
    order = [0]
    for k, near in ((1, 1 - u), (2, 2), (3, 3)):
        order.append(near + side * (3 - 2 * near))

    def head_peer(d):
        return (s, lax.rem(z + d, 4))

    def yc_peer(d):
        return (s_base + lax.rem(yc + d, 8), z)

    def zx_peer(d):
        return (lax.rem(zx + d, 16) * 8 + yc, z)

    up = (lax.rem(s + 1, 128), z)
    down = (lax.rem(s + 127, 128), z)

    x = lax.rem(zx, 4)
    barrier = pltpu.get_barrier_semaphore()

    def signal(sem, peer):
        pl.semaphore_signal(sem, inc=1, device_id=peer, device_id_type=MESH)

    def from_lead(x_at, yc_at, z_at):
        return (x_at - z_at) * (x_at - z_at) + (yc_at - z_at) * (yc_at - z_at)

    def x_peer(d):
        return ((zx - x + lax.rem(x + d, 4)) * 8 + yc, z)

    def far_lead(d):
        return (lax.rem(zx + 4 * d, 16) * 8 + yc, z)

    greeted = [(head_peer(d), from_lead(x, yc, lax.rem(z + d, 4))) for d in range(1, 4)]
    greeted += [(yc_peer(d), from_lead(x, lax.rem(yc + d, 8), z)) for d in range(1, 8)]
    greeted += [(x_peer(d), from_lead(lax.rem(x + d, 4), yc, z)) for d in range(1, 4)]
    mine = from_lead(x, yc, z)
    for peer, gap in greeted:
        @pl.when(gap != 0)
        def _():
            signal(barrier, peer)

    loads = []

    def load(src, dst):
        copy = pltpu.make_async_copy(src, dst, in_sem.at[len(loads)])
        copy.start()
        loads.append(copy)
        return copy

    c_tok = [load(tok.at[pl.ds(48 * i, 48)], X.at[z, i]) for i in range(2)]
    c_gain = load(gain, gain_v)
    c_qkv = []
    for h in range(3):
        q_at, k_at, v_at = (64, 64, 0) if h == 0 else (0, 0, 64)
        c_qkv.append(load(wqkv.at[pl.ds(64 * h, 64)], WQ.at[pl.ds(128 * h + q_at, 64)]))
        c_qkv.append(load(wqkv.at[pl.ds(192 + 64 * h, 64)], WQ.at[pl.ds(384 + 128 * h + k_at, 64)]))
        c_qkv.append(load(wqkv.at[pl.ds(384 + 64 * h, 64)], WQ.at[pl.ds(384 + 128 * h + v_at, 64)]))
    c_late = [load(wdec, WD)]
    for g in range(4):
        c_late.append(load(wout.at[pl.ds(192 * g, 128)], W01.at[pl.ds(128 * g, 128)]))
        c_late.append(load(wout.at[pl.ds(192 * g + 128, 64)], W2.at[0, pl.ds(128 * g, 64)]))
        c_late.append(load(wout.at[pl.ds(192 * g + 128, 64)], W2.at[1, pl.ds(128 * g + 64, 64)]))
    zero64 = jnp.zeros((64, 768), BF16)
    for h in range(3):
        WQ[pl.ds(128 * h + (0 if h == 0 else 64), 64), :] = zero64
    for g in range(4):
        W2[0, pl.ds(128 * g + 64, 64), :] = zero64
        W2[1, pl.ds(128 * g, 64), :] = zero64
    S4F[...] = jnp.zeros_like(S4F)
    Q4F[...] = jnp.zeros_like(Q4F)
    QF[:, 384:416, :] = jnp.zeros((6, 32, 128), F32)

    for copy in c_tok:
        copy.wait()

    @pl.when(mine != 0)
    def _():
        pl.semaphore_wait(barrier, len(greeted))

    for peer, gap in greeted:
        @pl.when(gap == 0)
        def _():
            signal(lead_sem, peer)

    @pl.when(mine == 0)
    def _():
        pl.semaphore_wait(lead_sem, len(greeted))
        for d in range(1, 4):
            signal(barrier, far_lead(d))

    def remote(src, dst, ssem, rsem, peer):
        return pltpu.make_async_remote_copy(
            src_ref=src, dst_ref=dst, send_sem=ssem, recv_sem=rsem,
            device_id=peer, device_id_type=MESH,
        )

    def own_copy(buf, ssem, rsem, way, p):
        peer = inner if way == 0 else outer
        return remote(buf.at[z, p], buf.at[z, p], ssem.at[way, p], rsem.at[z, p], peer)

    def own_send(buf, ssem, rsem, p):
        own_copy(buf, ssem, rsem, 0, p).start()

        @pl.when(u == 1)
        def _():
            own_copy(buf, ssem, rsem, 1, p).start()

    def pass_copy(buf, fsem, rsem, k, p):
        c = order[k]
        peer = inner if k == 1 else outer
        return remote(buf.at[c, p], buf.at[c, p], fsem.at[k, p], rsem.at[c, p], peer)

    def line_sent(buf, ssem, fsem, rsem, pieces):
        for p in range(pieces):
            own_copy(buf, ssem, rsem, 0, p).wait_send()

        @pl.when(u == 1)
        def _():
            for p in range(pieces):
                own_copy(buf, ssem, rsem, 1, p).wait_send()
                for k in range(1, 4):
                    pass_copy(buf, fsem, rsem, k, p).wait_send()

    sent = []

    for p in range(2):
        own_send(X, tok_s, tok_r, p)

    c_gain.wait()
    for copy in c_qkv:
        copy.wait()
    gain_row = gain_v[...][None, :]
    o2 = [off[0, 3 * z + h] for h in range(3)]
    o3 = [off[1, 3 * z + h] for h in range(3)]
    o4 = [off[2, 3 * z + h] for h in range(3)]
    row16 = lax.broadcasted_iota(jnp.int32, (16, 128), 0)
    zero8 = jnp.zeros((8, 128), F32)

    def near_copy(c, d):
        peer = (s_base + quad_base + lax.rem(quad + d, 4), z)
        return remote(BX.at[yc, c], BX.at[yc, c], bx_s.at[d], bx_r.at[d], peer)

    def far_copy(c, j):
        peer = (s_base + far_base + lax.rem(quad + j, 4), z)
        piece = BX.at[yc, c, pl.ds(96, 48)]
        return remote(piece, piece, bx_s.at[4 + j], bx_r.at[4 + j], peer)

    for k in range(4):
        c = z if k == 0 else order[k]
        if k:
            for p in range(2):
                arriving = pass_copy(X, tok_f, tok_r, k, p)
                arriving.wait_recv()

                @pl.when(u == 1)
                def _():
                    arriving.start()

        normed = layer_norm(X[c].reshape(96, 768), gain_row)
        rows = pl.ds(pl.multiple_of(c * 96, 96), 96)
        every = nt_dot(normed, WQ[...]).astype(BF16)
        for t in range(6):
            part = every[:, 128 * t : 128 * t + 128]
            QB[t, rows, :] = part
            QF[t, rows, :] = part.astype(F32)
        for h in range(3):
            two = QF[3 + h, pl.ds(c * 96 + o2[h], 24, stride=4), :]
            BX[yc, c, 32 * h : 32 * h + 32, :] = jnp.concatenate([two, zero8], 0).astype(BF16)
            three = QF[3 + h, pl.ds(c * 96 + o3[h], 16, stride=8), :]
            BX[yc, c, 96 + 16 * h : 112 + 16 * h, :] = jnp.where(row16 < 12, three, 0.0).astype(BF16)
        for d in range(1, 4):
            near_copy(c, d).start()
        for j in range(4):
            far_copy(c, j).start()

    lane = lax.broadcasted_iota(jnp.int32, (1, 128), 1)
    left = lane < 64
    right = lane >= 64
    out_lanes = (left, right, right)

    for h in range(3):
        for j in range(3):
            S4F[3 * h + j : 3 * h + j + 1, :] = QF[3 + h, pl.ds(o4[h] + 128 * j, 1), :]
            Q4F[3 * h + j : 3 * h + j + 1, :] = QF[h, pl.ds(o4[h] + 128 * j, 1), :]
    G1[zx] = S4F[...].astype(BF16)

    @pl.when(mine == 0)
    def _():
        pl.semaphore_wait(barrier, 3)
        for d in range(1, 4):
            signal(go_sem, x_peer(d))
        for d in range(1, 8):
            signal(go_sem, yc_peer(d))

    def branch_one(h):
        kv = QB[3 + h]
        for i in range(3):
            rows = pl.ds(128 * i, 128)
            T1[h, rows, :] = attend(QB[h, rows, :], kv, out_lanes[h])

    branch_one(0)
    branch_one(1)

    @pl.when(mine != 0)
    def _():
        pl.semaphore_wait(go_sem, 1)

        @pl.when(yc == z)
        def _():
            for d in range(1, 8):
                signal(go_sem, yc_peer(d))

    g1_copies = [
        remote(G1.at[zx], G1.at[zx], g1_s.at[d], g1_r.at[d], zx_peer(d)) for d in range(1, 16)
    ]
    for copy in g1_copies:
        copy.start()
    sent += g1_copies

    branch_one(2)

    for d in range(1, 4):
        src = quad_base + lax.rem(quad - d + 4, 4)
        remote(BX.at[src], BX.at[src], bx_s.at[d], bx_r.at[d], inner).wait_recv()
    for j in range(4):
        src = far_base + lax.rem(quad - j + 4, 4)
        piece = BX.at[src, :, pl.ds(96, 48)]
        remote(piece, piece, bx_s.at[4 + j], bx_r.at[4 + j], inner).wait_recv()

    key = lax.broadcasted_iota(jnp.int32, (1, 512), 1)
    full2 = (key & 31) < 24
    full3 = (key & 15) < 12

    def branch_two(h):
        kv = jnp.concatenate(
            [BX[quad_base + m, c, 32 * h : 32 * h + 32, :] for m in range(4) for c in range(4)], axis=0
        )
        q = QF[h, pl.ds(o2[h], 96, stride=4), :].astype(BF16)
        tile = attend(q, kv, out_lanes[h], full2)
        for p in range(4):
            E2[h, pl.ds(p, 96, stride=4), :] = tile

    def branch_three(h):
        kv = jnp.concatenate(
            [BX[m, c, 96 + 16 * h : 112 + 16 * h, :] for m in range(8) for c in range(4)], axis=0
        )
        q = QF[h, pl.ds(o3[h], 48, stride=8), :].astype(BF16)
        tile = attend(q, kv, out_lanes[h], full3)
        for p in range(8):
            E3[h, pl.ds(p, 48, stride=8), :] = tile

    token = lax.broadcasted_iota(jnp.int32, (384, 128), 0)

    def merge(h):
        t1, t2, t3 = T1[h], E2[h], E3[h]
        l1, l2, l3 = (pltpu.roll(t, 64, 1) for t in (t1, t2, t3))
        c2 = (token & 3) == o2[h]
        c3 = (token & 7) == o3[h]
        peak = jnp.where(c2, jnp.maximum(l1, l2), l1)
        peak = jnp.where(c3, jnp.maximum(peak, l3), peak)
        w1 = jnp.exp2(l1 - peak)
        w2 = jnp.where(c2, jnp.exp2(l2 - peak), 0.0)
        w3 = jnp.where(c3, jnp.exp2(l3 - peak), 0.0)
        den = w1 + w2 + w3
        out = (w1 * t1 + w2 * t2 + w3 * t3) / den
        lse = peak + jnp.log(den) * LOG2E
        MR[h] = jnp.where(out_lanes[h], out, pltpu.roll(lse, 64, 1))
        return out

    for h in range(2):
        branch_two(h)
        branch_three(h)
    m01 = jnp.where(left, merge(0), merge(1)).astype(BF16)
    for p in range(2):
        AA[z, p] = m01[192 * p : 192 * p + 192]
        own_send(AA, aa_s, aa_r, p)
    branch_two(2)
    branch_three(2)
    m2 = merge(2)
    AA[z, 2] = jnp.where(left, pltpu.roll(m2[:192], 64, 1), m2[192:]).astype(BF16)
    own_send(AA, aa_s, aa_r, 2)

    @pl.when(u == 1)
    def _():
        for k, p in [(2, p) for p in range(3)]:
            arriving = pass_copy(AA, aa_f, aa_r, k, p)
            arriving.wait_recv()
            arriving.start()

    for d in range(1, 16):
        src = lax.rem(zx - d + 16, 16)
        remote(G1.at[src], G1.at[src], g1_s.at[d], g1_r.at[d], zx_peer(d)).wait_recv()
    row_to = lax.broadcasted_iota(jnp.int32, (144, 256), 0)
    row_from = lax.broadcasted_iota(jnp.int32, (144, 256), 1)
    ninth = (row_to * 7282) >> 16
    pick = (row_from == row_to + 7 * ninth).astype(F32).astype(BF16)
    G2[yc] = jnp.dot(pick, G1[...].reshape(256, 128), preferred_element_type=F32).astype(BF16)
    g2_copies = [
        remote(G2.at[yc], G2.at[yc], g2_s.at[d], g2_r.at[d], yc_peer(d)) for d in range(1, 8)
    ]
    for copy in g2_copies:
        copy.start()
    sent += g2_copies

    @pl.when(u == 1)
    def _():
        for k, p in [(k, p) for p in range(3) for k in (1, 3)]:
            arriving = pass_copy(AA, aa_f, aa_r, k, p)
            arriving.wait_recv()
            arriving.start()

    for d in range(1, 8):
        src = lax.rem(yc - d + 8, 8)
        remote(G2.at[src], G2.at[src], g2_s.at[d], g2_r.at[d], yc_peer(d)).wait_recv()
    kv4 = G2[...].reshape(1152, 128)
    key4 = lax.broadcasted_iota(jnp.int32, (1, 1152), 1)
    key_at = key4 - 9 * ((key4 * 7282) >> 16)
    query4 = lax.broadcasted_iota(jnp.int32, (16, 1), 0)

    def head_row(r):
        return jnp.where(r < 3, 0, jnp.where(r < 6, 1, jnp.where(r < 9, 2, 3)))

    keep = head_row(key_at) == head_row(query4)
    lane16 = lax.broadcasted_iota(jnp.int32, (16, 128), 1)
    out16 = (row16 < 3) == (lane16 < 64)
    tile4 = attend(Q4F[...].astype(BF16), kv4, out16, keep)
    for h in range(3):
        for j in range(3):
            S4F[3 * h + j : 3 * h + j + 1, :] = MR[h, pl.ds(o4[h] + 128 * j, 1), :]
    tile1 = S4F[...]
    l1 = pltpu.roll(tile1, 64, 1)
    l4 = pltpu.roll(tile4, 64, 1)
    peak = jnp.maximum(l1, l4)
    w1 = jnp.exp2(l1 - peak)
    w4 = jnp.exp2(l4 - peak)
    both = (w1 * tile1 + w4 * tile4) / (w1 + w4)
    turned = pltpu.roll(both, 64, 1)
    PF[...] = jnp.zeros_like(PF)
    PF[0:3, :] = jnp.where(left, both[0:3], both[3:6])
    PF[3:6, :] = jnp.where(left, turned[6:9], both[6:9])
    PT[z] = PF[...].astype(BF16)
    pt_copies = [
        remote(PT.at[z], PT.at[z], pt_s.at[d], pt_r.at[d], head_peer(d)) for d in range(1, 4)
    ]
    for copy in pt_copies:
        copy.start()
    sent += pt_copies

    for copy in c_late:
        copy.wait()

    @pl.when(u == 0)
    def _():
        for k in range(1, 4):
            for p in range(3):
                pass_copy(AA, aa_f, aa_r, k, p).wait_recv()

    for d in range(1, 4):
        src = lax.rem(z - d + 4, 4)
        remote(PT.at[src], PT.at[src], pt_s.at[d], pt_r.at[d], head_peer(d)).wait_recv()
    tok192 = lax.broadcasted_iota(jnp.int32, (192, 128), 0)
    tok_packed = tok192 + jnp.where(left, 0, 192)
    pieces = []
    for g in range(4):
        patch = PT[g].astype(F32)
        o01 = jnp.where(left, off[2, 3 * g], off[2, 3 * g + 1])
        places = (
            (tok192, o01, 0, (0, 1)), (tok192 + 192, o01, 0, (1, 2)),
            (tok_packed, off[2, 3 * g + 2], 3, (0, 1, 2)),
        )
        fixed = []
        for p, (at, offset, first, groups) in enumerate(places):
            piece = AA[g, p].astype(F32)
            for j in groups:
                piece = jnp.where(at == offset + 128 * j, patch[first + j : first + j + 1], piece)
            fixed.append(piece.astype(BF16))
        pieces.append(fixed)
    for half in range(2):
        first = jnp.concatenate([pieces[g][half] for g in range(4)], axis=1)
        second = jnp.concatenate([pieces[g][2] for g in range(4)], axis=1)
        acc = jnp.dot(first, W01[...], preferred_element_type=F32)
        acc = acc + jnp.dot(second, W2[half], preferred_element_type=F32)
        own = X[2 * half : 2 * half + 2].reshape(192, 768).astype(F32)
        L[192 * half : 192 * half + 192, :] = (own + acc).astype(BF16)
    c_layer = pltpu.make_async_copy(
        L.at[pl.ds(pl.multiple_of(z * 96, 96), 96)], layer_out, out_sem.at[0]
    )
    c_layer.start()

    col = lax.broadcasted_iota(jnp.int32, (64, 384), 1)

    def part(dy):
        p = nt_dot(WD[192 * dy : 192 * dy + 192, :], L[...])
        before = jnp.where(col == 0, 0.0, pltpu.roll(p[0:64], 1, 1))
        after = jnp.where(col == 383, 0.0, pltpu.roll(p[128:192], 383, 1))
        return before + p[64:128] + after

    HS[0] = part(0).astype(BF16)
    h_up = remote(HS.at[0], HR.at[0], h_s.at[0], h_r.at[0], up)
    h_up.start()
    HS[1] = part(2).astype(BF16)
    h_down = remote(HS.at[1], HR.at[1], h_s.at[1], h_r.at[1], down)
    h_down.start()
    middle = part(1)
    line_sent(X, tok_s, tok_f, tok_r, 2)
    line_sent(AA, aa_s, aa_f, aa_r, 3)
    for d in range(1, 4):
        remote(BX.at[yc], BX.at[yc], bx_s.at[d], bx_r.at[d], inner).wait_send()
    for j in range(4):
        piece = BX.at[yc, :, pl.ds(96, 48)]
        remote(piece, piece, bx_s.at[4 + j], bx_r.at[4 + j], inner).wait_send()
    for copy in sent:
        copy.wait_send()
    h_up.wait_recv()
    h_down.wait_recv()
    conv = middle + jnp.where(s > 0, HR[0].astype(F32), 0.0)
    conv = conv + jnp.where(s < 127, HR[1].astype(F32), 0.0)
    DO[...] = (0.5 * conv * (1.0 + lax.erf(conv * 0.7071067811865476))).astype(BF16)
    c_dec = pltpu.make_async_copy(DO, dec_out, out_sem.at[1])
    c_dec.start()
    h_up.wait_send()
    h_down.wait_send()
    c_layer.wait()
    c_dec.wait()


def shards(tokens, norm_gain, qkv_weight, out_weight, dec_weight, offsets):
    wqkv = qkv_weight.reshape(576, 768)
    wdec = jnp.transpose(dec_weight, (1, 2, 0, 3)).reshape(576, 768)
    vm = pltpu.VMEM
    dma = pltpu.SemaphoreType.DMA
    layer, decoded = pl.pallas_call(
        body,
        out_shape=(
            jax.ShapeDtypeStruct((96, 768), BF16),
            jax.ShapeDtypeStruct((64, 384), BF16),
        ),
        in_specs=[pl.BlockSpec(memory_space=pl.ANY)] * 5
        + [pl.BlockSpec(memory_space=pltpu.SMEM)],
        out_specs=(pl.BlockSpec(memory_space=pl.ANY),) * 2,
        scratch_shapes=[
            vm((4, 2, 48, 768), BF16),
            vm((768,), F32),
            vm((768, 768), BF16),
            vm((512, 768), BF16),
            vm((2, 512, 768), BF16),
            vm((576, 768), BF16),
            vm((6, 384, 128), BF16),
            vm((6, 416, 128), F32),
            vm((8, 4, 144, 128), BF16),
            vm((16, 128), F32),
            vm((16, 128), F32),
            vm((16, 16, 128), BF16),
            vm((8, 144, 128), BF16),
            vm((3, 384, 128), F32),
            vm((3, 384, 128), F32),
            vm((3, 384, 128), F32),
            vm((3, 384, 128), F32),
            vm((4, 3, 192, 128), BF16),
            vm((16, 128), F32),
            vm((4, 16, 128), BF16),
            vm((384, 768), BF16),
            vm((2, 64, 384), BF16),
            vm((2, 64, 384), BF16),
            vm((64, 384), BF16),
            dma((26,)),
            dma((2, 2)), dma((4, 2)), dma((4, 2)),
            dma((8,)), dma((8,)),
            dma((16,)), dma((16,)),
            dma((8,)), dma((8,)),
            dma((2, 3)), dma((4, 3)), dma((4, 3)),
            dma((4,)), dma((4,)),
            dma((2,)), dma((2,)),
            dma((2,)),
            pltpu.SemaphoreType.REGULAR, pltpu.SemaphoreType.REGULAR,
        ],
        compiler_params=pltpu.CompilerParams(
            collective_id=0, has_side_effects=True, vmem_limit_bytes=60 * 1024 * 1024
        ),
        cost_estimate=pl.CostEstimate(
            flops=1500000000, bytes_accessed=4000000, transcendentals=700000
        ),
        name="dilated_layer",
    )(tokens, norm_gain, wqkv, out_weight, wdec, offsets)
    return layer, decoded.reshape(64, 1, 384)


def solution(mesh):
    placed = (
        P(("seq", "head"), None),
        P(),
        P(None, "head", None, None),
        P(),
        P("head", None, None, None),
        P(),
    )
    return jax.shard_map(
        shards,
        mesh=mesh,
        in_specs=placed,
        out_specs=(P(("seq", "head"), None), P("head", "seq", None)),
        check_vma=False,
    )
```

```python
import functools

import jax
import jax.numpy as jnp
from jax import lax
from jax.experimental import pallas as pl
from jax.experimental.pallas import tpu as pltpu
from jax.sharding import PartitionSpec as P

MESH = pl.DeviceIdType.MESH
LOG2E = 1.4426950408889634
SCALE = 0.125 * LOG2E
F32 = jnp.float32
BF16 = jnp.bfloat16


def nt_dot(a, b):
    return lax.dot_general(a, b, (((1,), (1,)), ((), ())), preferred_element_type=F32)


def seq_of(zh, x, y, c):
    return ((zh * 4 + x) * 4 + y) * 2 + c


def layer_norm(rows, gain):
    values = rows.astype(F32)
    centred = values - jnp.mean(values, -1, keepdims=True)
    spread = jnp.mean(centred * centred, -1, keepdims=True)
    return (centred * lax.rsqrt(spread + 1e-06) * gain).astype(BF16)


def attend(q, kv, out_lanes, keep=None):
    scores = nt_dot(q, kv) * SCALE
    if keep is not None:
        scores = jnp.where(keep, scores, -1e30)
    top = jnp.max(scores, -1, keepdims=True)
    terms = jnp.exp2(scores - top)
    total = jnp.sum(terms, -1, keepdims=True)
    out = jnp.dot(terms.astype(BF16), kv, preferred_element_type=F32)
    lse = top + jnp.log(total) * LOG2E
    return jnp.where(out_lanes, out / total, lse)


def body(
    tok, gain, wqkv, wout, wdec, off,
    layer_out, dec_out,
    X, gain_v, WQ, W01, W2, WD, QB, QF,
    BX, S4F, Q4F, G1, G2,
    T1, E2, E3, MR, AA, PF, PT, L, HS, HR,
    in_sem, tok_s, tok_f, tok_r, bx_s, bx_r, g1_s, g1_r, g2_s, g2_r,
    aa_s, aa_f, aa_r, pt_s, pt_r, h_s, h_r, lead_sem, go_sem,
):
    s = lax.axis_index("seq")
    z = lax.axis_index("head")
    yc = lax.rem(s, 8)
    zx = lax.div(s, 8)
    quad = lax.rem(s, 4)
    quad_base = yc - quad
    far_base = lax.rem(quad_base + 4, 8)
    s_base = s - yc
    side = lax.div(z, 2)
    u = z + side * (3 - 2 * z)
    inner = (s, z + 1 - 2 * side)
    outer = (s, z - 1 + 2 * side)
    order = [0]
    for k, near in ((1, 1 - u), (2, 2), (3, 3)):
        order.append(near + side * (3 - 2 * near))

    def head_peer(d):
        return (s, lax.rem(z + d, 4))

    def yc_peer(d):
        return (s_base + lax.rem(yc + d, 8), z)

    def zx_peer(d):
        return (lax.rem(zx + d, 16) * 8 + yc, z)

    up = (lax.rem(s + 1, 128), z)
    down = (lax.rem(s + 127, 128), z)

    x = lax.rem(zx, 4)
    barrier = pltpu.get_barrier_semaphore()

    def signal(sem, peer):
        pl.semaphore_signal(sem, inc=1, device_id=peer, device_id_type=MESH)

    def from_lead(x_at, yc_at, z_at):
        return (x_at - z_at) * (x_at - z_at) + (yc_at - z_at) * (yc_at - z_at)

    def x_peer(d):
        return ((zx - x + lax.rem(x + d, 4)) * 8 + yc, z)

    def far_lead(d):
        return (lax.rem(zx + 4 * d, 16) * 8 + yc, z)

    greeted = [(head_peer(d), from_lead(x, yc, lax.rem(z + d, 4))) for d in range(1, 4)]
    greeted += [(yc_peer(d), from_lead(x, lax.rem(yc + d, 8), z)) for d in range(1, 8)]
    greeted += [(x_peer(d), from_lead(lax.rem(x + d, 4), yc, z)) for d in range(1, 4)]
    mine = from_lead(x, yc, z)
    for peer, gap in greeted:
        @pl.when(gap != 0)
        def _():
            signal(barrier, peer)

    loads = []

    def load(src, dst):
        copy = pltpu.make_async_copy(src, dst, in_sem.at[len(loads)])
        copy.start()
        loads.append(copy)
        return copy

    c_tok = [load(tok.at[pl.ds(48 * i, 48)], X.at[z, i]) for i in range(2)]
    c_gain = load(gain, gain_v)
    c_qkv = []
    for h in range(3):
        q_at, k_at, v_at = (64, 64, 0) if h == 0 else (0, 0, 64)
        c_qkv.append(load(wqkv.at[pl.ds(64 * h, 64)], WQ.at[pl.ds(128 * h + q_at, 64)]))
        c_qkv.append(load(wqkv.at[pl.ds(192 + 64 * h, 64)], WQ.at[pl.ds(384 + 128 * h + k_at, 64)]))
        c_qkv.append(load(wqkv.at[pl.ds(384 + 64 * h, 64)], WQ.at[pl.ds(384 + 128 * h + v_at, 64)]))
    c_late = [load(wdec, WD)]
    for g in range(4):
        c_late.append(load(wout.at[pl.ds(192 * g, 128)], W01.at[pl.ds(128 * g, 128)]))
        c_late.append(load(wout.at[pl.ds(192 * g + 128, 64)], W2.at[0, pl.ds(128 * g, 64)]))
        c_late.append(load(wout.at[pl.ds(192 * g + 128, 64)], W2.at[1, pl.ds(128 * g + 64, 64)]))
    zero64 = jnp.zeros((64, 768), BF16)
    for h in range(3):
        WQ[pl.ds(128 * h + (0 if h == 0 else 64), 64), :] = zero64
    for g in range(4):
        W2[0, pl.ds(128 * g + 64, 64), :] = zero64
        W2[1, pl.ds(128 * g, 64), :] = zero64
    S4F[...] = jnp.zeros_like(S4F)
    Q4F[...] = jnp.zeros_like(Q4F)
    QF[:, 384:416, :] = jnp.zeros((6, 32, 128), F32)

    for copy in c_tok:
        copy.wait()

    @pl.when(mine != 0)
    def _():
        pl.semaphore_wait(barrier, len(greeted))

    for peer, gap in greeted:
        @pl.when(gap == 0)
        def _():
            signal(lead_sem, peer)

    @pl.when(mine == 0)
    def _():
        pl.semaphore_wait(lead_sem, len(greeted))
        for d in range(1, 4):
            signal(barrier, far_lead(d))

    def remote(src, dst, ssem, rsem, peer):
        return pltpu.make_async_remote_copy(
            src_ref=src, dst_ref=dst, send_sem=ssem, recv_sem=rsem,
            device_id=peer, device_id_type=MESH,
        )

    def own_copy(buf, ssem, rsem, way, p):
        peer = inner if way == 0 else outer
        return remote(buf.at[z, p], buf.at[z, p], ssem.at[way, p], rsem.at[z, p], peer)

    def own_send(buf, ssem, rsem, p):
        own_copy(buf, ssem, rsem, 0, p).start()

        @pl.when(u == 1)
        def _():
            own_copy(buf, ssem, rsem, 1, p).start()

    def pass_copy(buf, fsem, rsem, k, p):
        c = order[k]
        peer = inner if k == 1 else outer
        return remote(buf.at[c, p], buf.at[c, p], fsem.at[k, p], rsem.at[c, p], peer)

    def line_sent(buf, ssem, fsem, rsem, pieces):
        for p in range(pieces):
            own_copy(buf, ssem, rsem, 0, p).wait_send()

        @pl.when(u == 1)
        def _():
            for p in range(pieces):
                own_copy(buf, ssem, rsem, 1, p).wait_send()
                for k in range(1, 4):
                    pass_copy(buf, fsem, rsem, k, p).wait_send()

    sent = []

    for p in range(2):
        own_send(X, tok_s, tok_r, p)

    c_gain.wait()
    for copy in c_qkv:
        copy.wait()
    gain_row = gain_v[...][None, :]
    o2 = [off[0, 3 * z + h] for h in range(3)]
    o3 = [off[1, 3 * z + h] for h in range(3)]
    o4 = [off[2, 3 * z + h] for h in range(3)]
    row16 = lax.broadcasted_iota(jnp.int32, (16, 128), 0)
    zero8 = jnp.zeros((8, 128), F32)

    def near_copy(c, d):
        peer = (s_base + quad_base + lax.rem(quad + d, 4), z)
        return remote(BX.at[yc, c], BX.at[yc, c], bx_s.at[d], bx_r.at[d], peer)

    def far_copy(c, j):
        peer = (s_base + far_base + lax.rem(quad + j, 4), z)
        piece = BX.at[yc, c, pl.ds(96, 48)]
        return remote(piece, piece, bx_s.at[4 + j], bx_r.at[4 + j], peer)

    for k in range(4):
        c = z if k == 0 else order[k]
        if k == 3:

            @pl.when(mine == 0)
            def _():
                pl.semaphore_wait(barrier, 3)
                for d in range(1, 4):
                    signal(go_sem, x_peer(d))
                for d in range(1, 8):
                    signal(go_sem, yc_peer(d))

        if k:
            for p in range(2):
                arriving = pass_copy(X, tok_f, tok_r, k, p)
                arriving.wait_recv()

                @pl.when(u == 1)
                def _():
                    arriving.start()

        normed = layer_norm(X[c].reshape(96, 768), gain_row)
        rows = pl.ds(pl.multiple_of(c * 96, 96), 96)
        every = nt_dot(normed, WQ[...]).astype(BF16)
        for t in range(6):
            part = every[:, 128 * t : 128 * t + 128]
            QB[t, rows, :] = part
            QF[t, rows, :] = part.astype(F32)
        for h in range(3):
            two = QF[3 + h, pl.ds(c * 96 + o2[h], 24, stride=4), :]
            BX[yc, c, 32 * h : 32 * h + 32, :] = jnp.concatenate([two, zero8], 0).astype(BF16)
            three = QF[3 + h, pl.ds(c * 96 + o3[h], 16, stride=8), :]
            BX[yc, c, 96 + 16 * h : 112 + 16 * h, :] = jnp.where(row16 < 12, three, 0.0).astype(BF16)
        for d in range(1, 4):
            near_copy(c, d).start()
        for j in range(4):
            far_copy(c, j).start()

    lane = lax.broadcasted_iota(jnp.int32, (1, 128), 1)
    left = lane < 64
    right = lane >= 64
    out_lanes = (left, right, right)

    for h in range(3):
        for j in range(3):
            S4F[3 * h + j : 3 * h + j + 1, :] = QF[3 + h, pl.ds(o4[h] + 128 * j, 1), :]
            Q4F[3 * h + j : 3 * h + j + 1, :] = QF[h, pl.ds(o4[h] + 128 * j, 1), :]
    G1[zx] = S4F[...].astype(BF16)

    def branch_one(h):
        kv = QB[3 + h]
        for i in range(3):
            rows = pl.ds(128 * i, 128)
            T1[h, rows, :] = attend(QB[h, rows, :], kv, out_lanes[h])

    @pl.when(yc == z)
    def _():
        @pl.when(x != z)
        def _():
            pl.semaphore_wait(go_sem, 1)
            for d in range(1, 8):
                signal(go_sem, yc_peer(d))

    branch_one(0)
    branch_one(1)

    @pl.when(yc != z)
    def _():
        pl.semaphore_wait(go_sem, 1)

    g1_copies = [
        remote(G1.at[zx], G1.at[zx], g1_s.at[d], g1_r.at[d], zx_peer(d)) for d in range(1, 16)
    ]
    for copy in g1_copies:
        copy.start()
    sent += g1_copies

    branch_one(2)

    for d in range(1, 4):
        src = quad_base + lax.rem(quad - d + 4, 4)
        remote(BX.at[src], BX.at[src], bx_s.at[d], bx_r.at[d], inner).wait_recv()
    for j in range(4):
        src = far_base + lax.rem(quad - j + 4, 4)
        piece = BX.at[src, :, pl.ds(96, 48)]
        remote(piece, piece, bx_s.at[4 + j], bx_r.at[4 + j], inner).wait_recv()

    key = lax.broadcasted_iota(jnp.int32, (1, 512), 1)
    full2 = (key & 31) < 24
    full3 = (key & 15) < 12

    def branch_two(h):
        kv = jnp.concatenate(
            [BX[quad_base + m, c, 32 * h : 32 * h + 32, :] for m in range(4) for c in range(4)], axis=0
        )
        q = QF[h, pl.ds(o2[h], 96, stride=4), :].astype(BF16)
        tile = attend(q, kv, out_lanes[h], full2)
        for p in range(4):
            E2[h, pl.ds(p, 96, stride=4), :] = tile

    def branch_three(h):
        kv = jnp.concatenate(
            [BX[m, c, 96 + 16 * h : 112 + 16 * h, :] for m in range(8) for c in range(4)], axis=0
        )
        q = QF[h, pl.ds(o3[h], 48, stride=8), :].astype(BF16)
        tile = attend(q, kv, out_lanes[h], full3)
        for p in range(8):
            E3[h, pl.ds(p, 48, stride=8), :] = tile

    token = lax.broadcasted_iota(jnp.int32, (384, 128), 0)

    def merge(h):
        t1, t2, t3 = T1[h], E2[h], E3[h]
        l1, l2, l3 = (pltpu.roll(t, 64, 1) for t in (t1, t2, t3))
        c2 = (token & 3) == o2[h]
        c3 = (token & 7) == o3[h]
        peak = jnp.where(c2, jnp.maximum(l1, l2), l1)
        peak = jnp.where(c3, jnp.maximum(peak, l3), peak)
        w1 = jnp.exp2(l1 - peak)
        w2 = jnp.where(c2, jnp.exp2(l2 - peak), 0.0)
        w3 = jnp.where(c3, jnp.exp2(l3 - peak), 0.0)
        den = w1 + w2 + w3
        out = (w1 * t1 + w2 * t2 + w3 * t3) / den
        lse = peak + jnp.log(den) * LOG2E
        MR[h] = jnp.where(out_lanes[h], out, pltpu.roll(lse, 64, 1))
        return out

    for h in range(2):
        branch_two(h)
        branch_three(h)
    m01 = jnp.where(left, merge(0), merge(1)).astype(BF16)
    for p in range(2):
        AA[z, p] = m01[192 * p : 192 * p + 192]
        own_send(AA, aa_s, aa_r, p)

    branch_two(2)
    branch_three(2)
    m2 = merge(2)
    AA[z, 2] = jnp.where(left, pltpu.roll(m2[:192], 64, 1), m2[192:]).astype(BF16)
    own_send(AA, aa_s, aa_r, 2)

    @pl.when(u == 1)
    def _():
        for k, p in [(2, p) for p in range(3)]:
            arriving = pass_copy(AA, aa_f, aa_r, k, p)
            arriving.wait_recv()
            arriving.start()

    for d in range(1, 16):
        src = lax.rem(zx - d + 16, 16)
        remote(G1.at[src], G1.at[src], g1_s.at[d], g1_r.at[d], zx_peer(d)).wait_recv()
    row_to = lax.broadcasted_iota(jnp.int32, (144, 256), 0)
    row_from = lax.broadcasted_iota(jnp.int32, (144, 256), 1)
    ninth = (row_to * 7282) >> 16
    pick = (row_from == row_to + 7 * ninth).astype(F32).astype(BF16)
    G2[yc] = jnp.dot(pick, G1[...].reshape(256, 128), preferred_element_type=F32).astype(BF16)
    g2_copies = [
        remote(G2.at[yc], G2.at[yc], g2_s.at[d], g2_r.at[d], yc_peer(d)) for d in range(1, 8)
    ]
    for copy in g2_copies:
        copy.start()
    sent += g2_copies

    @pl.when(u == 1)
    def _():
        for k, p in [(k, p) for p in range(3) for k in (1, 3)]:
            arriving = pass_copy(AA, aa_f, aa_r, k, p)
            arriving.wait_recv()
            arriving.start()

    for d in range(1, 8):
        src = lax.rem(yc - d + 8, 8)
        remote(G2.at[src], G2.at[src], g2_s.at[d], g2_r.at[d], yc_peer(d)).wait_recv()
    kv4 = G2[...].reshape(1152, 128)
    key4 = lax.broadcasted_iota(jnp.int32, (1, 1152), 1)
    key_at = key4 - 9 * ((key4 * 7282) >> 16)
    query4 = lax.broadcasted_iota(jnp.int32, (16, 1), 0)

    def head_row(r):
        return jnp.where(r < 3, 0, jnp.where(r < 6, 1, jnp.where(r < 9, 2, 3)))

    keep = head_row(key_at) == head_row(query4)
    lane16 = lax.broadcasted_iota(jnp.int32, (16, 128), 1)
    out16 = (row16 < 3) == (lane16 < 64)
    tile4 = attend(Q4F[...].astype(BF16), kv4, out16, keep)
    for h in range(3):
        for j in range(3):
            S4F[3 * h + j : 3 * h + j + 1, :] = MR[h, pl.ds(o4[h] + 128 * j, 1), :]
    tile1 = S4F[...]
    l1 = pltpu.roll(tile1, 64, 1)
    l4 = pltpu.roll(tile4, 64, 1)
    peak = jnp.maximum(l1, l4)
    w1 = jnp.exp2(l1 - peak)
    w4 = jnp.exp2(l4 - peak)
    both = (w1 * tile1 + w4 * tile4) / (w1 + w4)
    turned = pltpu.roll(both, 64, 1)
    PF[...] = jnp.zeros_like(PF)
    PF[0:3, :] = jnp.where(left, both[0:3], both[3:6])
    PF[3:6, :] = jnp.where(left, turned[6:9], both[6:9])
    PT[z] = PF[...].astype(BF16)
    pt_copies = [
        remote(PT.at[z], PT.at[z], pt_s.at[d], pt_r.at[d], head_peer(d)) for d in range(1, 4)
    ]
    for copy in pt_copies:
        copy.start()
    sent += pt_copies

    for copy in c_late:
        copy.wait()

    @pl.when(u == 0)
    def _():
        for k in range(1, 4):
            for p in range(3):
                pass_copy(AA, aa_f, aa_r, k, p).wait_recv()

    for d in range(1, 4):
        src = lax.rem(z - d + 4, 4)
        remote(PT.at[src], PT.at[src], pt_s.at[d], pt_r.at[d], head_peer(d)).wait_recv()
    tok192 = lax.broadcasted_iota(jnp.int32, (192, 128), 0)
    tok_packed = tok192 + jnp.where(left, 0, 192)
    pieces = []
    for g in range(4):
        patch = PT[g].astype(F32)
        o01 = jnp.where(left, off[2, 3 * g], off[2, 3 * g + 1])
        places = (
            (tok192, o01, 0, (0, 1)), (tok192 + 192, o01, 0, (1, 2)),
            (tok_packed, off[2, 3 * g + 2], 3, (0, 1, 2)),
        )
        fixed = []
        for p, (at, offset, first, groups) in enumerate(places):
            piece = AA[g, p].astype(F32)
            for j in groups:
                piece = jnp.where(at == offset + 128 * j, patch[first + j : first + j + 1], piece)
            fixed.append(piece.astype(BF16))
        pieces.append(fixed)
    for half in range(2):
        first = jnp.concatenate([pieces[g][half] for g in range(4)], axis=1)
        second = jnp.concatenate([pieces[g][2] for g in range(4)], axis=1)
        acc = jnp.dot(first, W01[...], preferred_element_type=F32)
        acc = acc + jnp.dot(second, W2[half], preferred_element_type=F32)
        own = X[2 * half : 2 * half + 2].reshape(192, 768).astype(F32)
        L[192 * half : 192 * half + 192, :] = (own + acc).astype(BF16)

    col = lax.broadcasted_iota(jnp.int32, (64, 384), 1)

    def part(dy):
        p = nt_dot(WD[192 * dy : 192 * dy + 192, :], L[...])
        before = jnp.where(col == 0, 0.0, pltpu.roll(p[0:64], 1, 1))
        after = jnp.where(col == 383, 0.0, pltpu.roll(p[128:192], 383, 1))
        return before + p[64:128] + after

    HS[0] = part(0).astype(BF16)
    h_up = remote(HS.at[0], HR.at[0], h_s.at[0], h_r.at[0], up)

    @pl.when(s < 127)
    def _():
        h_up.start()

    HS[1] = part(2).astype(BF16)
    h_down = remote(HS.at[1], HR.at[1], h_s.at[1], h_r.at[1], down)

    @pl.when(s > 0)
    def _():
        h_down.start()

    layer_out[...] = L[pl.ds(pl.multiple_of(z * 96, 96), 96), :]
    middle = part(1)
    line_sent(X, tok_s, tok_f, tok_r, 2)
    line_sent(AA, aa_s, aa_f, aa_r, 3)
    for d in range(1, 4):
        remote(BX.at[yc], BX.at[yc], bx_s.at[d], bx_r.at[d], inner).wait_send()
    for j in range(4):
        piece = BX.at[yc, :, pl.ds(96, 48)]
        remote(piece, piece, bx_s.at[4 + j], bx_r.at[4 + j], inner).wait_send()
    for copy in sent:
        copy.wait_send()

    @pl.when(s > 0)
    def _():
        h_up.wait_recv()
        h_down.wait_send()

    @pl.when(s < 127)
    def _():
        h_down.wait_recv()
        h_up.wait_send()

    conv = middle + jnp.where(s > 0, HR[0].astype(F32), 0.0)
    conv = conv + jnp.where(s < 127, HR[1].astype(F32), 0.0)
    dec_out[...] = (0.5 * conv * (1.0 + lax.erf(conv * 0.7071067811865476))).astype(BF16)


def shards(tokens, norm_gain, qkv_weight, out_weight, dec_weight, offsets):
    wqkv = qkv_weight.reshape(576, 768)
    wdec = jnp.transpose(dec_weight, (1, 2, 0, 3)).reshape(576, 768)
    vm = pltpu.VMEM
    dma = pltpu.SemaphoreType.DMA
    layer, decoded = pl.pallas_call(
        body,
        out_shape=(
            pltpu.VMEM((96, 768), BF16),
            pltpu.VMEM((64, 384), BF16),
        ),
        in_specs=[pl.BlockSpec(memory_space=pl.ANY)] * 5
        + [pl.BlockSpec(memory_space=pltpu.SMEM)],
        out_specs=(pl.BlockSpec(memory_space=pltpu.VMEM),) * 2,
        scratch_shapes=[
            vm((4, 2, 48, 768), BF16),
            vm((768,), F32),
            vm((768, 768), BF16),
            vm((512, 768), BF16),
            vm((2, 512, 768), BF16),
            vm((576, 768), BF16),
            vm((6, 384, 128), BF16),
            vm((6, 416, 128), F32),
            vm((8, 4, 144, 128), BF16),
            vm((16, 128), F32),
            vm((16, 128), F32),
            vm((16, 16, 128), BF16),
            vm((8, 144, 128), BF16),
            vm((3, 384, 128), F32),
            vm((3, 384, 128), F32),
            vm((3, 384, 128), F32),
            vm((3, 384, 128), F32),
            vm((4, 3, 192, 128), BF16),
            vm((16, 128), F32),
            vm((4, 16, 128), BF16),
            vm((384, 768), BF16),
            vm((2, 64, 384), BF16),
            vm((2, 64, 384), BF16),
            dma((26,)),
            dma((2, 2)), dma((4, 2)), dma((4, 2)),
            dma((8,)), dma((8,)),
            dma((16,)), dma((16,)),
            dma((8,)), dma((8,)),
            dma((2, 3)), dma((4, 3)), dma((4, 3)),
            dma((4,)), dma((4,)),
            dma((2,)), dma((2,)),
            pltpu.SemaphoreType.REGULAR, pltpu.SemaphoreType.REGULAR,
        ],
        compiler_params=pltpu.CompilerParams(
            collective_id=0, has_side_effects=True, vmem_limit_bytes=60 * 1024 * 1024
        ),
        cost_estimate=pl.CostEstimate(
            flops=1500000000, bytes_accessed=4000000, transcendentals=700000
        ),
        name="dilated_layer",
    )(tokens, norm_gain, wqkv, out_weight, wdec, offsets)
    return layer, decoded.reshape(64, 1, 384)


def solution(mesh):
    placed = (
        P(("seq", "head"), None),
        P(),
        P(None, "head", None, None),
        P(),
        P("head", None, None, None),
        P(),
    )
    return jax.shard_map(
        shards,
        mesh=mesh,
        in_specs=placed,
        out_specs=(P(("seq", "head"), None), P("head", "seq", None)),
        check_vma=False,
    )
```

```python
import functools

import jax
import jax.numpy as jnp
from jax import lax
from jax.experimental import pallas as pl
from jax.experimental.pallas import tpu as pltpu
from jax.sharding import PartitionSpec as P

MESH = pl.DeviceIdType.MESH
LOG2E = 1.4426950408889634
SCALE = 0.125 * LOG2E
F32 = jnp.float32
BF16 = jnp.bfloat16


def nt_dot(a, b):
    return lax.dot_general(a, b, (((1,), (1,)), ((), ())), preferred_element_type=F32)


def seq_of(zh, x, y, c):
    return ((zh * 4 + x) * 4 + y) * 2 + c


def layer_norm(rows, gain):
    values = rows.astype(F32)
    centred = values - jnp.mean(values, -1, keepdims=True)
    spread = jnp.mean(centred * centred, -1, keepdims=True)
    return (centred * lax.rsqrt(spread + 1e-06) * gain).astype(BF16)


def attend(q, kv, out_lanes, keep=None):
    scores = nt_dot(q, kv) * SCALE
    if keep is not None:
        scores = jnp.where(keep, scores, -1e30)
    top = jnp.max(scores, -1, keepdims=True)
    terms = jnp.exp2(scores - top)
    total = jnp.sum(terms, -1, keepdims=True)
    out = jnp.dot(terms.astype(BF16), kv, preferred_element_type=F32)
    lse = top + jnp.log(total) * LOG2E
    return jnp.where(out_lanes, out / total, lse)


def body(
    tok, gain, wqkv, wout, wdec, off,
    layer_out, dec_out,
    X, gain_v, WQ, W01, W2, WD, QB, QF,
    BX, S4F, Q4F, G1, G2,
    T1, E2, E3, MR, AA, PF, PT, L, HS, HR,
    in_sem, tok_s, tok_f, tok_r, bx_s, bx_r, g1_s, g1_r, g2_s, g2_r,
    aa_s, aa_f, aa_r, pt_s, pt_r, h_s, h_r, lead_sem, go_sem,
):
    s = lax.axis_index("seq")
    z = lax.axis_index("head")
    yc = lax.rem(s, 8)
    zx = lax.div(s, 8)
    quad = lax.rem(s, 4)
    quad_base = yc - quad
    far_base = lax.rem(quad_base + 4, 8)
    s_base = s - yc
    side = lax.div(z, 2)
    u = z + side * (3 - 2 * z)
    inner = (s, z + 1 - 2 * side)
    outer = (s, z - 1 + 2 * side)
    order = [0]
    for k, near in ((1, 1 - u), (2, 2), (3, 3)):
        order.append(near + side * (3 - 2 * near))

    def head_peer(d):
        return (s, lax.rem(z + d, 4))

    def yc_peer(d):
        return (s_base + lax.rem(yc + d, 8), z)

    def zx_peer(d):
        return (lax.rem(zx + d, 16) * 8 + yc, z)

    up = (lax.rem(s + 1, 128), z)
    down = (lax.rem(s + 127, 128), z)

    x = lax.rem(zx, 4)
    zh = lax.div(zx, 4)
    barrier = pltpu.get_barrier_semaphore()

    def signal(sem, peer):
        pl.semaphore_signal(sem, inc=1, device_id=peer, device_id_type=MESH)

    def from_lead(x_at, yc_at, z_at):
        return (x_at - z_at) * (x_at - z_at) + (yc_at - z_at - 2) * (yc_at - z_at - 2)

    def x_peer(d):
        return ((zx - x + lax.rem(x + d, 4)) * 8 + yc, z)

    def far_lead(d):
        return (lax.rem(zx + 4 * d, 16) * 8 + yc, z)

    greeted = [(head_peer(d), from_lead(x, yc, lax.rem(z + d, 4))) for d in range(1, 4)]
    greeted += [(yc_peer(d), from_lead(x, lax.rem(yc + d, 8), z)) for d in range(1, 8)]
    greeted += [(x_peer(d), from_lead(lax.rem(x + d, 4), yc, z)) for d in range(1, 4)]
    mine = from_lead(x, yc, z)
    for peer, gap in greeted:
        @pl.when(gap != 0)
        def _():
            signal(barrier, peer)

    loads = []

    def load(src, dst):
        copy = pltpu.make_async_copy(src, dst, in_sem.at[len(loads)])
        copy.start()
        loads.append(copy)
        return copy

    c_tok = [load(tok.at[pl.ds(48 * i, 48)], X.at[z, i]) for i in range(2)]
    c_gain = load(gain, gain_v)
    c_qkv = []
    for h in range(3):
        q_at, k_at, v_at = (64, 64, 0) if h == 0 else (0, 0, 64)
        c_qkv.append(load(wqkv.at[pl.ds(64 * h, 64)], WQ.at[pl.ds(128 * h + q_at, 64)]))
        c_qkv.append(load(wqkv.at[pl.ds(192 + 64 * h, 64)], WQ.at[pl.ds(384 + 128 * h + k_at, 64)]))
        c_qkv.append(load(wqkv.at[pl.ds(384 + 64 * h, 64)], WQ.at[pl.ds(384 + 128 * h + v_at, 64)]))
    c_late = [load(wdec, WD)]
    for g in range(4):
        c_late.append(load(wout.at[pl.ds(192 * g, 128)], W01.at[pl.ds(128 * g, 128)]))
        c_late.append(load(wout.at[pl.ds(192 * g + 128, 64)], W2.at[0, pl.ds(128 * g, 64)]))
        c_late.append(load(wout.at[pl.ds(192 * g + 128, 64)], W2.at[1, pl.ds(128 * g + 64, 64)]))
    zero64 = jnp.zeros((64, 768), BF16)
    for h in range(3):
        WQ[pl.ds(128 * h + (0 if h == 0 else 64), 64), :] = zero64
    for g in range(4):
        W2[0, pl.ds(128 * g + 64, 64), :] = zero64
        W2[1, pl.ds(128 * g, 64), :] = zero64
    S4F[...] = jnp.zeros_like(S4F)
    Q4F[...] = jnp.zeros_like(Q4F)
    QF[:, 384:416, :] = jnp.zeros((6, 32, 128), F32)

    for copy in c_tok:
        copy.wait()

    @pl.when(mine != 0)
    def _():
        pl.semaphore_wait(barrier, len(greeted))

    for peer, gap in greeted:
        @pl.when(gap == 0)
        def _():
            signal(lead_sem, peer)

    @pl.when(mine == 0)
    def _():
        pl.semaphore_wait(lead_sem, len(greeted))
        for d in range(1, 4):
            signal(barrier, far_lead(d))

    def remote(src, dst, ssem, rsem, peer):
        return pltpu.make_async_remote_copy(
            src_ref=src, dst_ref=dst, send_sem=ssem, recv_sem=rsem,
            device_id=peer, device_id_type=MESH,
        )

    def own_copy(buf, ssem, rsem, way, p):
        peer = inner if way == 0 else outer
        return remote(buf.at[z, p], buf.at[z, p], ssem.at[way, p], rsem.at[z, p], peer)

    def own_send(buf, ssem, rsem, p):
        own_copy(buf, ssem, rsem, 0, p).start()

        @pl.when(u == 1)
        def _():
            own_copy(buf, ssem, rsem, 1, p).start()

    def pass_copy(buf, fsem, rsem, k, p):
        c = order[k]
        peer = inner if k == 1 else outer
        return remote(buf.at[c, p], buf.at[c, p], fsem.at[k, p], rsem.at[c, p], peer)

    def line_sent(buf, ssem, fsem, rsem, pieces):
        for p in range(pieces):
            own_copy(buf, ssem, rsem, 0, p).wait_send()

        @pl.when(u == 1)
        def _():
            for p in range(pieces):
                own_copy(buf, ssem, rsem, 1, p).wait_send()
                for k in range(1, 4):
                    pass_copy(buf, fsem, rsem, k, p).wait_send()

    sent = []

    for p in range(2):
        own_send(X, tok_s, tok_r, p)

    c_gain.wait()
    for copy in c_qkv:
        copy.wait()
    gain_row = gain_v[...][None, :]
    o2 = [off[0, 3 * z + h] for h in range(3)]
    o3 = [off[1, 3 * z + h] for h in range(3)]
    o4 = [off[2, 3 * z + h] for h in range(3)]
    row16 = lax.broadcasted_iota(jnp.int32, (16, 128), 0)
    zero8 = jnp.zeros((8, 128), F32)

    def near_copy(c, d):
        peer = (s_base + quad_base + lax.rem(quad + d, 4), z)
        return remote(BX.at[yc, c], BX.at[yc, c], bx_s.at[d], bx_r.at[d], peer)

    def far_copy(c, j):
        peer = (s_base + far_base + lax.rem(quad + j, 4), z)
        piece = BX.at[yc, c, pl.ds(96, 48)]
        return remote(piece, piece, bx_s.at[4 + j], bx_r.at[4 + j], peer)

    def lead_word():
        @pl.when(mine == 0)
        def _():
            pl.semaphore_wait(barrier, 3)
            for d in range(1, 4):
                signal(go_sem, x_peer(d))
            for d in range(1, 8):
                signal(go_sem, yc_peer(d))

    def head_word():
        @pl.when(yc == z + 2)
        def _():
            @pl.when(x != z)
            def _():
                pl.semaphore_wait(go_sem, 1)
                for d in range(1, 8):
                    signal(go_sem, yc_peer(d))

    for k in range(4):
        c = z if k == 0 else order[k]
        if k == 3:

            @pl.when(zh != 0)
            def _():
                lead_word()

        if k:
            for p in range(2):
                arriving = pass_copy(X, tok_f, tok_r, k, p)
                arriving.wait_recv()

                @pl.when(u == 1)
                def _():
                    arriving.start()

        normed = layer_norm(X[c].reshape(96, 768), gain_row)
        rows = pl.ds(pl.multiple_of(c * 96, 96), 96)
        every = nt_dot(normed, WQ[...]).astype(BF16)
        for t in range(6):
            part = every[:, 128 * t : 128 * t + 128]
            QB[t, rows, :] = part
            QF[t, rows, :] = part.astype(F32)
        for h in range(3):
            two = QF[3 + h, pl.ds(c * 96 + o2[h], 24, stride=4), :]
            BX[yc, c, 32 * h : 32 * h + 32, :] = jnp.concatenate([two, zero8], 0).astype(BF16)
            three = QF[3 + h, pl.ds(c * 96 + o3[h], 16, stride=8), :]
            BX[yc, c, 96 + 16 * h : 112 + 16 * h, :] = jnp.where(row16 < 12, three, 0.0).astype(BF16)
        for d in range(1, 4):
            near_copy(c, d).start()
        for j in range(4):
            far_copy(c, j).start()

    lane = lax.broadcasted_iota(jnp.int32, (1, 128), 1)
    left = lane < 64
    right = lane >= 64
    out_lanes = (left, right, right)

    for h in range(3):
        for j in range(3):
            S4F[3 * h + j : 3 * h + j + 1, :] = QF[3 + h, pl.ds(o4[h] + 128 * j, 1), :]
            Q4F[3 * h + j : 3 * h + j + 1, :] = QF[h, pl.ds(o4[h] + 128 * j, 1), :]
    G1[zx] = S4F[...].astype(BF16)

    def branch_one(h):
        kv = QB[3 + h]
        for i in range(3):
            rows = pl.ds(128 * i, 128)
            T1[h, rows, :] = attend(QB[h, rows, :], kv, out_lanes[h])

    g1_copies = [
        remote(G1.at[zx], G1.at[zx], g1_s.at[d], g1_r.at[d], zx_peer(d)) for d in range(1, 16)
    ]
    sent += g1_copies

    def row_word():
        @pl.when(yc != z + 2)
        def _():
            pl.semaphore_wait(go_sem, 1)

        for copy in g1_copies:
            copy.start()

    @pl.when(zh != 0)
    def _():
        head_word()

    @pl.when(zh == 0)
    def _():
        lead_word()

    branch_one(0)
    branch_one(1)

    @pl.when(zh == 0)
    def _():
        head_word()

    @pl.when(zh != 0)
    def _():
        row_word()

    branch_one(2)


    for d in range(1, 4):
        src = quad_base + lax.rem(quad - d + 4, 4)
        remote(BX.at[src], BX.at[src], bx_s.at[d], bx_r.at[d], inner).wait_recv()
    for j in range(4):
        src = far_base + lax.rem(quad - j + 4, 4)
        piece = BX.at[src, :, pl.ds(96, 48)]
        remote(piece, piece, bx_s.at[4 + j], bx_r.at[4 + j], inner).wait_recv()

    key = lax.broadcasted_iota(jnp.int32, (1, 512), 1)
    full2 = (key & 31) < 24
    full3 = (key & 15) < 12

    def branch_two(h):
        kv = jnp.concatenate(
            [BX[quad_base + m, c, 32 * h : 32 * h + 32, :] for m in range(4) for c in range(4)], axis=0
        )
        q = QF[h, pl.ds(o2[h], 96, stride=4), :].astype(BF16)
        tile = attend(q, kv, out_lanes[h], full2)
        for p in range(4):
            E2[h, pl.ds(p, 96, stride=4), :] = tile

    def branch_three(h):
        kv = jnp.concatenate(
            [BX[m, c, 96 + 16 * h : 112 + 16 * h, :] for m in range(8) for c in range(4)], axis=0
        )
        q = QF[h, pl.ds(o3[h], 48, stride=8), :].astype(BF16)
        tile = attend(q, kv, out_lanes[h], full3)
        for p in range(8):
            E3[h, pl.ds(p, 48, stride=8), :] = tile

    token = lax.broadcasted_iota(jnp.int32, (384, 128), 0)

    def merge(h):
        t1, t2, t3 = T1[h], E2[h], E3[h]
        l1, l2, l3 = (pltpu.roll(t, 64, 1) for t in (t1, t2, t3))
        c2 = (token & 3) == o2[h]
        c3 = (token & 7) == o3[h]
        peak = jnp.where(c2, jnp.maximum(l1, l2), l1)
        peak = jnp.where(c3, jnp.maximum(peak, l3), peak)
        w1 = jnp.exp2(l1 - peak)
        w2 = jnp.where(c2, jnp.exp2(l2 - peak), 0.0)
        w3 = jnp.where(c3, jnp.exp2(l3 - peak), 0.0)
        den = w1 + w2 + w3
        out = (w1 * t1 + w2 * t2 + w3 * t3) / den
        lse = peak + jnp.log(den) * LOG2E
        MR[h] = jnp.where(out_lanes[h], out, pltpu.roll(lse, 64, 1))
        return out

    @pl.when(zh == 0)
    def _():
        row_word()

    for h in range(2):
        branch_two(h)
        branch_three(h)
    m01 = jnp.where(left, merge(0), merge(1)).astype(BF16)
    for p in range(2):
        AA[z, p] = m01[192 * p : 192 * p + 192]
        own_send(AA, aa_s, aa_r, p)

    branch_two(2)
    branch_three(2)
    m2 = merge(2)
    AA[z, 2] = jnp.where(left, pltpu.roll(m2[:192], 64, 1), m2[192:]).astype(BF16)
    own_send(AA, aa_s, aa_r, 2)

    @pl.when(u == 1)
    def _():
        for k, p in ((2, 0), (2, 1)):
            arriving = pass_copy(AA, aa_f, aa_r, k, p)
            arriving.wait_recv()
            arriving.start()

    for d in range(1, 16):
        src = lax.rem(zx - d + 16, 16)
        remote(G1.at[src], G1.at[src], g1_s.at[d], g1_r.at[d], zx_peer(d)).wait_recv()
    row_to = lax.broadcasted_iota(jnp.int32, (144, 256), 0)
    row_from = lax.broadcasted_iota(jnp.int32, (144, 256), 1)
    ninth = (row_to * 7282) >> 16
    pick = (row_from == row_to + 7 * ninth).astype(F32).astype(BF16)
    G2[yc] = jnp.dot(pick, G1[...].reshape(256, 128), preferred_element_type=F32).astype(BF16)
    g2_copies = [
        remote(G2.at[yc], G2.at[yc], g2_s.at[d], g2_r.at[d], yc_peer(d)) for d in range(1, 8)
    ]
    for copy in g2_copies:
        copy.start()
    sent += g2_copies

    @pl.when(u == 1)
    def _():
        for k, p in ((2, 2), (1, 0), (3, 0), (1, 1), (3, 1), (1, 2), (3, 2)):
            arriving = pass_copy(AA, aa_f, aa_r, k, p)
            arriving.wait_recv()
            arriving.start()

    for d in range(1, 8):
        src = lax.rem(yc - d + 8, 8)
        remote(G2.at[src], G2.at[src], g2_s.at[d], g2_r.at[d], yc_peer(d)).wait_recv()
    kv4 = G2[...].reshape(1152, 128)
    key4 = lax.broadcasted_iota(jnp.int32, (1, 1152), 1)
    key_at = key4 - 9 * ((key4 * 7282) >> 16)
    query4 = lax.broadcasted_iota(jnp.int32, (16, 1), 0)

    def head_row(r):
        return jnp.where(r < 3, 0, jnp.where(r < 6, 1, jnp.where(r < 9, 2, 3)))

    keep = head_row(key_at) == head_row(query4)
    lane16 = lax.broadcasted_iota(jnp.int32, (16, 128), 1)
    out16 = (row16 < 3) == (lane16 < 64)
    tile4 = attend(Q4F[...].astype(BF16), kv4, out16, keep)
    for h in range(3):
        for j in range(3):
            S4F[3 * h + j : 3 * h + j + 1, :] = MR[h, pl.ds(o4[h] + 128 * j, 1), :]
    tile1 = S4F[...]
    l1 = pltpu.roll(tile1, 64, 1)
    l4 = pltpu.roll(tile4, 64, 1)
    peak = jnp.maximum(l1, l4)
    w1 = jnp.exp2(l1 - peak)
    w4 = jnp.exp2(l4 - peak)
    both = (w1 * tile1 + w4 * tile4) / (w1 + w4)
    turned = pltpu.roll(both, 64, 1)
    PF[...] = jnp.zeros_like(PF)
    PF[0:3, :] = jnp.where(left, both[0:3], both[3:6])
    PF[3:6, :] = jnp.where(left, turned[6:9], both[6:9])
    PT[z] = PF[...].astype(BF16)
    pt_copies = [
        remote(PT.at[z], PT.at[z], pt_s.at[d], pt_r.at[d], head_peer(d)) for d in range(1, 4)
    ]
    for copy in pt_copies:
        copy.start()
    sent += pt_copies

    for copy in c_late:
        copy.wait()

    @pl.when(u == 0)
    def _():
        for k in range(1, 4):
            for p in range(3):
                pass_copy(AA, aa_f, aa_r, k, p).wait_recv()

    for d in range(1, 4):
        src = lax.rem(z - d + 4, 4)
        remote(PT.at[src], PT.at[src], pt_s.at[d], pt_r.at[d], head_peer(d)).wait_recv()
    tok192 = lax.broadcasted_iota(jnp.int32, (192, 128), 0)
    tok_packed = tok192 + jnp.where(left, 0, 192)
    pieces = []
    for g in range(4):
        patch = PT[g].astype(F32)
        o01 = jnp.where(left, off[2, 3 * g], off[2, 3 * g + 1])
        places = (
            (tok192, o01, 0, (0, 1)), (tok192 + 192, o01, 0, (1, 2)),
            (tok_packed, off[2, 3 * g + 2], 3, (0, 1, 2)),
        )
        fixed = []
        for p, (at, offset, first, groups) in enumerate(places):
            piece = AA[g, p].astype(F32)
            for j in groups:
                piece = jnp.where(at == offset + 128 * j, patch[first + j : first + j + 1], piece)
            fixed.append(piece.astype(BF16))
        pieces.append(fixed)
    for half in range(2):
        first = jnp.concatenate([pieces[g][half] for g in range(4)], axis=1)
        second = jnp.concatenate([pieces[g][2] for g in range(4)], axis=1)
        acc = jnp.dot(first, W01[...], preferred_element_type=F32)
        acc = acc + jnp.dot(second, W2[half], preferred_element_type=F32)
        own = X[2 * half : 2 * half + 2].reshape(192, 768).astype(F32)
        L[192 * half : 192 * half + 192, :] = (own + acc).astype(BF16)

    col = lax.broadcasted_iota(jnp.int32, (64, 384), 1)

    def part(dy):
        p = nt_dot(WD[192 * dy : 192 * dy + 192, :], L[...])
        before = jnp.where(col == 0, 0.0, pltpu.roll(p[0:64], 1, 1))
        after = jnp.where(col == 383, 0.0, pltpu.roll(p[128:192], 383, 1))
        return before + p[64:128] + after

    HS[1] = part(2).astype(BF16)
    h_down = remote(HS.at[1], HR.at[1], h_s.at[1], h_r.at[1], down)

    @pl.when(s > 0)
    def _():
        h_down.start()

    HS[0] = part(0).astype(BF16)
    h_up = remote(HS.at[0], HR.at[0], h_s.at[0], h_r.at[0], up)

    @pl.when(s < 127)
    def _():
        h_up.start()

    layer_out[...] = L[pl.ds(pl.multiple_of(z * 96, 96), 96), :]
    middle = part(1)
    line_sent(X, tok_s, tok_f, tok_r, 2)
    line_sent(AA, aa_s, aa_f, aa_r, 3)
    for d in range(1, 4):
        remote(BX.at[yc], BX.at[yc], bx_s.at[d], bx_r.at[d], inner).wait_send()
    for j in range(4):
        piece = BX.at[yc, :, pl.ds(96, 48)]
        remote(piece, piece, bx_s.at[4 + j], bx_r.at[4 + j], inner).wait_send()
    for copy in sent:
        copy.wait_send()

    @pl.when(s > 0)
    def _():
        h_up.wait_recv()
        h_down.wait_send()

    @pl.when(s < 127)
    def _():
        h_down.wait_recv()
        h_up.wait_send()

    conv = middle + jnp.where(s > 0, HR[0].astype(F32), 0.0)
    conv = conv + jnp.where(s < 127, HR[1].astype(F32), 0.0)
    dec_out[...] = (0.5 * conv * (1.0 + lax.erf(conv * 0.7071067811865476))).astype(BF16)


def shards(tokens, norm_gain, qkv_weight, out_weight, dec_weight, offsets):
    wqkv = qkv_weight.reshape(576, 768)
    wdec = jnp.transpose(dec_weight, (1, 2, 0, 3)).reshape(576, 768)
    vm = pltpu.VMEM
    dma = pltpu.SemaphoreType.DMA
    layer, decoded = pl.pallas_call(
        body,
        out_shape=(
            pltpu.VMEM((96, 768), BF16),
            pltpu.VMEM((64, 384), BF16),
        ),
        in_specs=[pl.BlockSpec(memory_space=pl.ANY)] * 5
        + [pl.BlockSpec(memory_space=pltpu.SMEM)],
        out_specs=(pl.BlockSpec(memory_space=pltpu.VMEM),) * 2,
        scratch_shapes=[
            vm((4, 2, 48, 768), BF16),
            vm((768,), F32),
            vm((768, 768), BF16),
            vm((512, 768), BF16),
            vm((2, 512, 768), BF16),
            vm((576, 768), BF16),
            vm((6, 384, 128), BF16),
            vm((6, 416, 128), F32),
            vm((8, 4, 144, 128), BF16),
            vm((16, 128), F32),
            vm((16, 128), F32),
            vm((16, 16, 128), BF16),
            vm((8, 144, 128), BF16),
            vm((3, 384, 128), F32),
            vm((3, 384, 128), F32),
            vm((3, 384, 128), F32),
            vm((3, 384, 128), F32),
            vm((4, 3, 192, 128), BF16),
            vm((16, 128), F32),
            vm((4, 16, 128), BF16),
            vm((384, 768), BF16),
            vm((2, 64, 384), BF16),
            vm((2, 64, 384), BF16),
            dma((26,)),
            dma((2, 2)), dma((4, 2)), dma((4, 2)),
            dma((8,)), dma((8,)),
            dma((16,)), dma((16,)),
            dma((8,)), dma((8,)),
            dma((2, 3)), dma((4, 3)), dma((4, 3)),
            dma((4,)), dma((4,)),
            dma((2,)), dma((2,)),
            pltpu.SemaphoreType.REGULAR, pltpu.SemaphoreType.REGULAR,
        ],
        compiler_params=pltpu.CompilerParams(
            collective_id=0, has_side_effects=True, vmem_limit_bytes=60 * 1024 * 1024
        ),
        cost_estimate=pl.CostEstimate(
            flops=1500000000, bytes_accessed=4000000, transcendentals=700000
        ),
        name="dilated_layer",
    )(tokens, norm_gain, wqkv, out_weight, wdec, offsets)
    return layer, decoded.reshape(64, 1, 384)


def solution(mesh):
    placed = (
        P(("seq", "head"), None),
        P(),
        P(None, "head", None, None),
        P(),
        P("head", None, None, None),
        P(),
    )
    return jax.shard_map(
        shards,
        mesh=mesh,
        in_specs=placed,
        out_specs=(P(("seq", "head"), None), P("head", "seq", None)),
        check_vma=False,
    )
```

```python
import functools

import jax
import jax.numpy as jnp
from jax import lax
from jax.experimental import pallas as pl
from jax.experimental.pallas import tpu as pltpu
from jax.sharding import PartitionSpec as P

MESH = pl.DeviceIdType.MESH
LOG2E = 1.4426950408889634
SCALE = 0.125 * LOG2E
F32 = jnp.float32
BF16 = jnp.bfloat16


def nt_dot(a, b):
    return lax.dot_general(a, b, (((1,), (1,)), ((), ())), preferred_element_type=F32)


def seq_of(zh, x, y, c):
    return ((zh * 4 + x) * 4 + y) * 2 + c


def layer_norm(rows, gain):
    values = rows.astype(F32)
    centred = values - jnp.mean(values, -1, keepdims=True)
    spread = jnp.mean(centred * centred, -1, keepdims=True)
    return (centred * lax.rsqrt(spread + 1e-06) * gain).astype(BF16)


def attend(q, kv, out_lanes, keep=None):
    scores = nt_dot(q, kv) * SCALE
    if keep is not None:
        scores = jnp.where(keep, scores, -1e30)
    top = jnp.max(scores, -1, keepdims=True)
    terms = jnp.exp2(scores - top)
    total = jnp.sum(terms, -1, keepdims=True)
    out = jnp.dot(terms.astype(BF16), kv, preferred_element_type=F32)
    lse = top + jnp.log(total) * LOG2E
    return jnp.where(out_lanes, out / total, lse)


def body(
    tok, gain, wqkv, wout, wdec, off,
    layer_out, dec_out,
    X, gain_v, WQ, W01, W2, WD, QB, QF,
    BX, S4F, Q4F, G1, G2,
    T1, E2, E3, MR, AA, PF, PT, L, HS, HR,
    in_sem, tok_s, tok_f, tok_r, bx_s, bx_r, g1_s, g1_r, g2_s, g2_r,
    aa_s, aa_f, aa_r, pt_s, pt_r, h_s, h_r, lead_sem, go_sem,
):
    s = lax.axis_index("seq")
    z = lax.axis_index("head")
    yc = lax.rem(s, 8)
    zx = lax.div(s, 8)
    quad = lax.rem(s, 4)
    quad_base = yc - quad
    far_base = lax.rem(quad_base + 4, 8)
    s_base = s - yc
    side = lax.div(z, 2)
    u = z + side * (3 - 2 * z)
    inner = (s, z + 1 - 2 * side)
    outer = (s, z - 1 + 2 * side)
    order = [0]
    for k, near in ((1, 1 - u), (2, 2), (3, 3)):
        order.append(near + side * (3 - 2 * near))

    def head_peer(d):
        return (s, lax.rem(z + d, 4))

    def yc_peer(d):
        return (s_base + lax.rem(yc + d, 8), z)

    def zx_peer(d):
        return (lax.rem(zx + d, 16) * 8 + yc, z)

    up = (lax.rem(s + 1, 128), z)
    down = (lax.rem(s + 127, 128), z)

    x = lax.rem(zx, 4)
    zh = lax.div(zx, 4)
    barrier = pltpu.get_barrier_semaphore()

    def signal(sem, peer):
        pl.semaphore_signal(sem, inc=1, device_id=peer, device_id_type=MESH)

    def from_lead(x_at, yc_at, z_at):
        return (x_at - z_at) * (x_at - z_at) + (yc_at - z_at - 2) * (yc_at - z_at - 2)

    def x_peer(d):
        return ((zx - x + lax.rem(x + d, 4)) * 8 + yc, z)

    def far_lead(d):
        return (lax.rem(zx + 4 * d, 16) * 8 + yc, z)

    greeted = [(head_peer(d), from_lead(x, yc, lax.rem(z + d, 4))) for d in range(1, 4)]
    greeted += [(yc_peer(d), from_lead(x, lax.rem(yc + d, 8), z)) for d in range(1, 8)]
    greeted += [(x_peer(d), from_lead(lax.rem(x + d, 4), yc, z)) for d in range(1, 4)]
    mine = from_lead(x, yc, z)
    for peer, gap in greeted:
        @pl.when(gap != 0)
        def _():
            signal(barrier, peer)

    loads = []

    def load(src, dst):
        copy = pltpu.make_async_copy(src, dst, in_sem.at[len(loads)])
        copy.start()
        loads.append(copy)
        return copy

    c_tok = [load(tok.at[pl.ds(48 * i, 48)], X.at[z, i]) for i in range(2)]
    c_gain = load(gain, gain_v)
    c_qkv = []
    for h in range(3):
        q_at, k_at, v_at = (64, 64, 0) if h == 0 else (0, 0, 64)
        c_qkv.append(load(wqkv.at[pl.ds(64 * h, 64)], WQ.at[pl.ds(128 * h + q_at, 64)]))
        c_qkv.append(load(wqkv.at[pl.ds(192 + 64 * h, 64)], WQ.at[pl.ds(384 + 128 * h + k_at, 64)]))
        c_qkv.append(load(wqkv.at[pl.ds(384 + 64 * h, 64)], WQ.at[pl.ds(384 + 128 * h + v_at, 64)]))
    c_late = [load(wdec, WD)]
    for g in range(4):
        c_late.append(load(wout.at[pl.ds(192 * g, 128)], W01.at[pl.ds(128 * g, 128)]))
        c_late.append(load(wout.at[pl.ds(192 * g + 128, 64)], W2.at[0, pl.ds(128 * g, 64)]))
        c_late.append(load(wout.at[pl.ds(192 * g + 128, 64)], W2.at[1, pl.ds(128 * g + 64, 64)]))
    zero64 = jnp.zeros((64, 768), BF16)
    for h in range(3):
        WQ[pl.ds(128 * h + (0 if h == 0 else 64), 64), :] = zero64
    for g in range(4):
        W2[0, pl.ds(128 * g + 64, 64), :] = zero64
        W2[1, pl.ds(128 * g, 64), :] = zero64
    S4F[...] = jnp.zeros_like(S4F)
    Q4F[...] = jnp.zeros_like(Q4F)
    QF[:, 384:424, :] = jnp.zeros((6, 40, 128), F32)

    for copy in c_tok:
        copy.wait()

    @pl.when(mine != 0)
    def _():
        pl.semaphore_wait(barrier, len(greeted))

    for peer, gap in greeted:
        @pl.when(gap == 0)
        def _():
            signal(lead_sem, peer)

    @pl.when(mine == 0)
    def _():
        pl.semaphore_wait(lead_sem, len(greeted))
        for d in range(1, 4):
            signal(barrier, far_lead(d))

    def remote(src, dst, ssem, rsem, peer):
        return pltpu.make_async_remote_copy(
            src_ref=src, dst_ref=dst, send_sem=ssem, recv_sem=rsem,
            device_id=peer, device_id_type=MESH,
        )

    def own_copy(buf, ssem, rsem, way, p):
        peer = inner if way == 0 else outer
        return remote(buf.at[z, p], buf.at[z, p], ssem.at[way, p], rsem.at[z, p], peer)

    def own_send(buf, ssem, rsem, p):
        own_copy(buf, ssem, rsem, 0, p).start()

        @pl.when(u == 1)
        def _():
            own_copy(buf, ssem, rsem, 1, p).start()

    def pass_copy(buf, fsem, rsem, k, p):
        c = order[k]
        peer = inner if k == 1 else outer
        return remote(buf.at[c, p], buf.at[c, p], fsem.at[k, p], rsem.at[c, p], peer)

    def line_sent(buf, ssem, fsem, rsem, pieces):
        for p in range(pieces):
            own_copy(buf, ssem, rsem, 0, p).wait_send()

        @pl.when(u == 1)
        def _():
            for p in range(pieces):
                own_copy(buf, ssem, rsem, 1, p).wait_send()
                for k in range(1, 4):
                    pass_copy(buf, fsem, rsem, k, p).wait_send()

    sent = []

    for p in range(2):
        own_send(X, tok_s, tok_r, p)

    c_gain.wait()
    for copy in c_qkv:
        copy.wait()
    gain_row = gain_v[...][None, :]
    o2 = [off[0, 3 * z + h] for h in range(3)]
    o3 = [off[1, 3 * z + h] for h in range(3)]
    o4 = [off[2, 3 * z + h] for h in range(3)]
    row16 = lax.broadcasted_iota(jnp.int32, (16, 128), 0)
    zero8 = jnp.zeros((8, 128), F32)

    def near_copy(c, d):
        peer = (s_base + quad_base + lax.rem(quad + d, 4), z)
        return remote(BX.at[yc, c], BX.at[yc, c], bx_s.at[d], bx_r.at[d], peer)

    def far_copy(c, j):
        peer = (s_base + far_base + lax.rem(quad + j, 4), z)
        piece = BX.at[yc, c, pl.ds(96, 48)]
        return remote(piece, piece, bx_s.at[4 + j], bx_r.at[4 + j], peer)

    def lead_word():
        @pl.when(mine == 0)
        def _():
            pl.semaphore_wait(barrier, 3)
            for d in range(1, 4):
                signal(go_sem, x_peer(d))
            for d in range(1, 8):
                signal(go_sem, yc_peer(d))

    def head_word():
        @pl.when(yc == z + 2)
        def _():
            @pl.when(x != z)
            def _():
                pl.semaphore_wait(go_sem, 1)
                for d in range(1, 8):
                    signal(go_sem, yc_peer(d))

    for k in range(4):
        c = z if k == 0 else order[k]
        if k == 3:

            @pl.when(zh != 0)
            def _():
                lead_word()

        if k:
            for p in range(2):
                arriving = pass_copy(X, tok_f, tok_r, k, p)
                arriving.wait_recv()

                @pl.when(u == 1)
                def _():
                    arriving.start()

        normed = layer_norm(X[c].reshape(96, 768), gain_row)
        rows = pl.ds(pl.multiple_of(c * 96, 96), 96)
        every = nt_dot(normed, WQ[...]).astype(BF16)
        for t in range(6):
            part = every[:, 128 * t : 128 * t + 128]
            QB[t, rows, :] = part
            QF[t, rows, :] = part.astype(F32)
        for h in range(3):
            two = QF[3 + h, pl.ds(c * 96 + o2[h], 24, stride=4), :]
            BX[yc, c, 32 * h : 32 * h + 32, :] = jnp.concatenate([two, zero8], 0).astype(BF16)
            three = QF[3 + h, pl.ds(c * 96 + o3[h], 16, stride=8), :]
            BX[yc, c, 96 + 16 * h : 112 + 16 * h, :] = jnp.where(row16 < 12, three, 0.0).astype(BF16)
        for d in range(1, 4):
            near_copy(c, d).start()
        for j in range(4):
            far_copy(c, j).start()

    lane = lax.broadcasted_iota(jnp.int32, (1, 128), 1)
    left = lane < 64
    right = lane >= 64
    out_lanes = (left, right, right)

    for h in range(3):
        for j in range(3):
            S4F[3 * h + j : 3 * h + j + 1, :] = QF[3 + h, pl.ds(o4[h] + 128 * j, 1), :]
            Q4F[3 * h + j : 3 * h + j + 1, :] = QF[h, pl.ds(o4[h] + 128 * j, 1), :]
    G1[zx] = S4F[...].astype(BF16)

    def branch_one(h):
        kv = QB[3 + h]
        for i in range(3):
            rows = pl.ds(128 * i, 128)
            T1[h, rows, :] = attend(QB[h, rows, :], kv, out_lanes[h])

    g1_copies = [
        remote(G1.at[zx], G1.at[zx], g1_s.at[d], g1_r.at[d], zx_peer(d)) for d in range(1, 16)
    ]
    sent += g1_copies

    def row_word():
        @pl.when(yc != z + 2)
        def _():
            pl.semaphore_wait(go_sem, 1)

        for copy in g1_copies:
            copy.start()

    @pl.when(zh != 0)
    def _():
        head_word()

    @pl.when(zh == 0)
    def _():
        lead_word()

    branch_one(0)
    branch_one(1)

    @pl.when(zh == 0)
    def _():
        head_word()

    @pl.when(zh != 0)
    def _():
        row_word()

    branch_one(2)


    for d in range(1, 4):
        src = quad_base + lax.rem(quad - d + 4, 4)
        remote(BX.at[src], BX.at[src], bx_s.at[d], bx_r.at[d], inner).wait_recv()
    for j in range(4):
        src = far_base + lax.rem(quad - j + 4, 4)
        piece = BX.at[src, :, pl.ds(96, 48)]
        remote(piece, piece, bx_s.at[4 + j], bx_r.at[4 + j], inner).wait_recv()

    key = lax.broadcasted_iota(jnp.int32, (1, 512), 1)
    full2 = (key & 31) < 24
    full3 = (key & 15) < 12

    def branch_two(h):
        kv = jnp.concatenate(
            [BX[quad_base + m, c, 32 * h : 32 * h + 32, :] for m in range(4) for c in range(4)], axis=0
        )
        q = QF[h, pl.ds(o2[h], 96, stride=4), :].astype(BF16)
        tile = attend(q, kv, out_lanes[h], full2)
        for p in range(4):
            E2[h, pl.ds(p, 96, stride=4), :] = tile

    def branch_three(h):
        kv = jnp.concatenate(
            [BX[m, c, 96 + 16 * h : 112 + 16 * h, :] for m in range(8) for c in range(4)], axis=0
        )
        q = QF[h, pl.ds(o3[h], 48, stride=8), :].astype(BF16)
        tile = attend(q, kv, out_lanes[h], full3)
        for p in range(8):
            E3[h, pl.ds(p, 48, stride=8), :] = tile

    token = lax.broadcasted_iota(jnp.int32, (384, 128), 0)

    def merge(h):
        t1, t2, t3 = T1[h], E2[h, 0:384, :], E3[h, 0:384, :]
        l1, l2, l3 = (pltpu.roll(t, 64, 1) for t in (t1, t2, t3))
        c2 = (token & 3) == o2[h]
        c3 = (token & 7) == o3[h]
        peak = jnp.where(c2, jnp.maximum(l1, l2), l1)
        peak = jnp.where(c3, jnp.maximum(peak, l3), peak)
        w1 = jnp.exp2(l1 - peak)
        w2 = jnp.where(c2, jnp.exp2(l2 - peak), 0.0)
        w3 = jnp.where(c3, jnp.exp2(l3 - peak), 0.0)
        den = w1 + w2 + w3
        out = (w1 * t1 + w2 * t2 + w3 * t3) / den
        lse = peak + jnp.log(den) * LOG2E
        MR[h] = jnp.where(out_lanes[h], out, pltpu.roll(lse, 64, 1))
        return out

    @pl.when(zh == 0)
    def _():
        row_word()

    for h in range(2):
        branch_two(h)
        branch_three(h)
    m01 = jnp.where(left, merge(0), merge(1)).astype(BF16)
    for p in range(2):
        AA[z, p] = m01[192 * p : 192 * p + 192]
        own_send(AA, aa_s, aa_r, p)

    branch_two(2)
    branch_three(2)
    m2 = merge(2)
    AA[z, 2] = jnp.where(left, pltpu.roll(m2[:192], 64, 1), m2[192:]).astype(BF16)
    own_send(AA, aa_s, aa_r, 2)

    @pl.when(u == 1)
    def _():
        for k, p in ((2, 0), (2, 1)):
            arriving = pass_copy(AA, aa_f, aa_r, k, p)
            arriving.wait_recv()
            arriving.start()

    for d in range(1, 16):
        src = lax.rem(zx - d + 16, 16)
        remote(G1.at[src], G1.at[src], g1_s.at[d], g1_r.at[d], zx_peer(d)).wait_recv()
    row_to = lax.broadcasted_iota(jnp.int32, (144, 256), 0)
    row_from = lax.broadcasted_iota(jnp.int32, (144, 256), 1)
    ninth = (row_to * 7282) >> 16
    pick = (row_from == row_to + 7 * ninth).astype(F32).astype(BF16)
    G2[yc] = jnp.dot(pick, G1[...].reshape(256, 128), preferred_element_type=F32).astype(BF16)
    g2_copies = [
        remote(G2.at[yc], G2.at[yc], g2_s.at[d], g2_r.at[d], yc_peer(d)) for d in range(1, 8)
    ]
    for copy in g2_copies:
        copy.start()
    sent += g2_copies

    @pl.when(u == 1)
    def _():
        for k, p in ((2, 2), (1, 0), (3, 0), (1, 1), (3, 1), (1, 2), (3, 2)):
            arriving = pass_copy(AA, aa_f, aa_r, k, p)
            arriving.wait_recv()
            arriving.start()

    for d in range(1, 8):
        src = lax.rem(yc - d + 8, 8)
        remote(G2.at[src], G2.at[src], g2_s.at[d], g2_r.at[d], yc_peer(d)).wait_recv()
    kv4 = G2[...].reshape(1152, 128)
    key4 = lax.broadcasted_iota(jnp.int32, (1, 1152), 1)
    key_at = key4 - 9 * ((key4 * 7282) >> 16)
    query4 = lax.broadcasted_iota(jnp.int32, (16, 1), 0)

    def head_row(r):
        return jnp.where(r < 3, 0, jnp.where(r < 6, 1, jnp.where(r < 9, 2, 3)))

    keep = head_row(key_at) == head_row(query4)
    lane16 = lax.broadcasted_iota(jnp.int32, (16, 128), 1)
    out16 = (row16 < 3) == (lane16 < 64)
    tile4 = attend(Q4F[...].astype(BF16), kv4, out16, keep)
    for h in range(3):
        for j in range(3):
            S4F[3 * h + j : 3 * h + j + 1, :] = MR[h, pl.ds(o4[h] + 128 * j, 1), :]
    tile1 = S4F[...]
    l1 = pltpu.roll(tile1, 64, 1)
    l4 = pltpu.roll(tile4, 64, 1)
    peak = jnp.maximum(l1, l4)
    w1 = jnp.exp2(l1 - peak)
    w4 = jnp.exp2(l4 - peak)
    both = (w1 * tile1 + w4 * tile4) / (w1 + w4)
    turned = pltpu.roll(both, 64, 1)
    PF[...] = jnp.zeros_like(PF)
    PF[0:3, :] = jnp.where(left, both[0:3], both[3:6])
    PF[3:6, :] = jnp.where(left, turned[6:9], both[6:9])
    PT[z] = PF[...].astype(BF16)
    pt_copies = [
        remote(PT.at[z], PT.at[z], pt_s.at[d], pt_r.at[d], head_peer(d)) for d in range(1, 4)
    ]
    for copy in pt_copies:
        copy.start()
    sent += pt_copies

    for copy in c_late:
        copy.wait()

    @pl.when(u == 0)
    def _():
        for k in range(1, 4):
            for p in range(3):
                pass_copy(AA, aa_f, aa_r, k, p).wait_recv()

    for d in range(1, 4):
        src = lax.rem(z - d + 4, 4)
        remote(PT.at[src], PT.at[src], pt_s.at[d], pt_r.at[d], head_peer(d)).wait_recv()
    tok192 = lax.broadcasted_iota(jnp.int32, (192, 128), 0)
    tok_packed = tok192 + jnp.where(left, 0, 192)
    pieces = []
    for g in range(4):
        patch = PT[g].astype(F32)
        o01 = jnp.where(left, off[2, 3 * g], off[2, 3 * g + 1])
        places = (
            (tok192, o01, 0, (0, 1)), (tok192 + 192, o01, 0, (1, 2)),
            (tok_packed, off[2, 3 * g + 2], 3, (0, 1, 2)),
        )
        fixed = []
        for p, (at, offset, first, groups) in enumerate(places):
            piece = AA[g, p].astype(F32)
            for j in groups:
                piece = jnp.where(at == offset + 128 * j, patch[first + j : first + j + 1], piece)
            fixed.append(piece.astype(BF16))
        pieces.append(fixed)
    for half in range(2):
        first = jnp.concatenate([pieces[g][half] for g in range(4)], axis=1)
        second = jnp.concatenate([pieces[g][2] for g in range(4)], axis=1)
        acc = jnp.dot(first, W01[...], preferred_element_type=F32)
        acc = acc + jnp.dot(second, W2[half], preferred_element_type=F32)
        own = X[2 * half : 2 * half + 2].reshape(192, 768).astype(F32)
        L[192 * half : 192 * half + 192, :] = (own + acc).astype(BF16)

    col = lax.broadcasted_iota(jnp.int32, (64, 384), 1)

    def part(dy):
        p = nt_dot(WD[192 * dy : 192 * dy + 192, :], L[...])
        before = jnp.where(col == 0, 0.0, pltpu.roll(p[0:64], 1, 1))
        after = jnp.where(col == 383, 0.0, pltpu.roll(p[128:192], 383, 1))
        return before + p[64:128] + after

    HS[1] = part(2).astype(BF16)
    h_down = remote(HS.at[1], HR.at[1], h_s.at[1], h_r.at[1], down)

    @pl.when(s > 0)
    def _():
        h_down.start()

    HS[0] = part(0).astype(BF16)
    h_up = remote(HS.at[0], HR.at[0], h_s.at[0], h_r.at[0], up)

    @pl.when(s < 127)
    def _():
        h_up.start()

    layer_out[...] = L[pl.ds(pl.multiple_of(z * 96, 96), 96), :]
    middle = part(1)
    line_sent(X, tok_s, tok_f, tok_r, 2)
    line_sent(AA, aa_s, aa_f, aa_r, 3)
    for d in range(1, 4):
        remote(BX.at[yc], BX.at[yc], bx_s.at[d], bx_r.at[d], inner).wait_send()
    for j in range(4):
        piece = BX.at[yc, :, pl.ds(96, 48)]
        remote(piece, piece, bx_s.at[4 + j], bx_r.at[4 + j], inner).wait_send()
    for copy in sent:
        copy.wait_send()

    @pl.when(s > 0)
    def _():
        h_up.wait_recv()
        h_down.wait_send()

    @pl.when(s < 127)
    def _():
        h_down.wait_recv()
        h_up.wait_send()

    conv = middle + jnp.where(s > 0, HR[0].astype(F32), 0.0)
    conv = conv + jnp.where(s < 127, HR[1].astype(F32), 0.0)
    dec_out[...] = (0.5 * conv * (1.0 + lax.erf(conv * 0.7071067811865476))).astype(BF16)


def shards(tokens, norm_gain, qkv_weight, out_weight, dec_weight, offsets):
    wqkv = qkv_weight.reshape(576, 768)
    wdec = jnp.transpose(dec_weight, (1, 2, 0, 3)).reshape(576, 768)
    vm = pltpu.VMEM
    dma = pltpu.SemaphoreType.DMA
    layer, decoded = pl.pallas_call(
        body,
        out_shape=(
            pltpu.VMEM((96, 768), BF16),
            pltpu.VMEM((64, 384), BF16),
        ),
        in_specs=[pl.BlockSpec(memory_space=pl.ANY)] * 5
        + [pl.BlockSpec(memory_space=pltpu.SMEM)],
        out_specs=(pl.BlockSpec(memory_space=pltpu.VMEM),) * 2,
        scratch_shapes=[
            vm((4, 2, 48, 768), BF16),
            vm((768,), F32),
            vm((768, 768), BF16),
            vm((512, 768), BF16),
            vm((2, 512, 768), BF16),
            vm((576, 768), BF16),
            vm((6, 384, 128), BF16),
            vm((6, 424, 128), F32),
            vm((8, 4, 144, 128), BF16),
            vm((16, 128), F32),
            vm((16, 128), F32),
            vm((16, 16, 128), BF16),
            vm((8, 144, 128), BF16),
            vm((3, 384, 128), F32),
            vm((3, 392, 128), F32),
            vm((3, 392, 128), F32),
            vm((3, 384, 128), F32),
            vm((4, 3, 192, 128), BF16),
            vm((16, 128), F32),
            vm((4, 16, 128), BF16),
            vm((384, 768), BF16),
            vm((2, 64, 384), BF16),
            vm((2, 64, 384), BF16),
            dma((26,)),
            dma((2, 2)), dma((4, 2)), dma((4, 2)),
            dma((8,)), dma((8,)),
            dma((16,)), dma((16,)),
            dma((8,)), dma((8,)),
            dma((2, 3)), dma((4, 3)), dma((4, 3)),
            dma((4,)), dma((4,)),
            dma((2,)), dma((2,)),
            pltpu.SemaphoreType.REGULAR, pltpu.SemaphoreType.REGULAR,
        ],
        compiler_params=pltpu.CompilerParams(
            collective_id=0, has_side_effects=True, vmem_limit_bytes=60 * 1024 * 1024
        ),
        cost_estimate=pl.CostEstimate(
            flops=1500000000, bytes_accessed=4000000, transcendentals=700000
        ),
        name="dilated_layer",
    )(tokens, norm_gain, wqkv, out_weight, wdec, offsets)
    return layer, decoded.reshape(64, 1, 384)


def solution(mesh):
    placed = (
        P(("seq", "head"), None),
        P(),
        P(None, "head", None, None),
        P(),
        P("head", None, None, None),
        P(),
    )
    return jax.shard_map(
        shards,
        mesh=mesh,
        in_specs=placed,
        out_specs=(P(("seq", "head"), None), P("head", "seq", None)),
        check_vma=False,
    )
```
